128 devices in a mesh: ctx: 32 (over z, y_lo, x), tp: 4 (over y_hi, core).
Axes of the slice: x: 4, y: 4 (y_hi: 2, y_lo: 2; y = y_hi * 2 + y_lo), z: 4, core: 2. Of those that a mesh axis runs over, the one named last changes fastest.
Arguments:
- q_nope: bfloat16 [4096, 64, 128], P('ctx', 'tp'), may hold values from -6 to 6
- q_rope: bfloat16 [4096, 64, 64], P('ctx', 'tp'), may hold values from -16 to 16
- latent: bfloat16 [4096, 576], P('ctx'), may hold values from -6 to 6
- up_keys: bfloat16 [64, 128, 512], P('tp'), may hold values from -0.25 to 0.25
- up_values: bfloat16 [64, 512, 128], P('tp'), may hold values from -1.5 to 1.5
- out_grad: bfloat16 [4096, 64, 128], P('ctx', 'tp'), may hold values from -6 to 6
Outputs:
- attn_out: bfloat16 [4096, 64, 128], P('ctx', 'tp')
- grad_q_nope: bfloat16 [4096, 64, 128], P('ctx', 'tp')
- grad_q_rope: bfloat16 [4096, 64, 64], P('ctx', 'tp')
- grad_latent: float32 [4096, 576], P('ctx')
The draws below stay inside these ranges and needn't reach their ends.
All inputs are finite; a program needn't handle non-finite values.
Results may differ from the reference program's by a relative error of at most 0.034.
Values may be sent and summed in bfloat16 or wider, within the bound.
A program may use at most 192 MiB of HBM per device.

```python
import jax
import jax.numpy as jnp
import numpy as np
from jax import lax

D_LAT = 512
D_ROPE = 64
HEAD_DIM = 128
HEADS = 64
ROWS = 128
SEQ = 4096
N_CTX = 32


def draw_q_rope(key, part):
    key = jax.random.fold_in(key, 11)
    values = jnp.clip(jax.random.normal(key, (SEQ, HEADS, D_ROPE), jnp.float32), -6.0, 6.0)
    return values.astype(jnp.bfloat16)


def draw_latent(key, part):
    key = jax.random.fold_in(key, 13)
    values = jnp.clip(jax.random.normal(key, (SEQ, D_LAT + D_ROPE), jnp.float32), -6.0, 6.0)
    return values.astype(jnp.bfloat16)


def block_levels(stream_key, shape, pieces, low, top_value):
    def one(axis_at, blocks):
        draws = jax.random.uniform(jax.random.fold_in(jax.random.fold_in(stream_key, 6), axis_at), (blocks,), jnp.float32, low / len(pieces), top_value / len(pieces))
        return jnp.repeat(jnp.exp(draws), shape[axis_at] // blocks).reshape((-1,) + (1,) * (len(shape) - axis_at - 1))

    gain = one(*pieces[0])
    for cut in pieces[1:]:
        gain = gain * one(*cut)
    return gain


def bell_draw(rng, shape, scale, bound, pieces=(), kind=jnp.bfloat16):
    array = scale * jax.random.normal(rng, shape, jnp.float32)
    if pieces:
        array = array * block_levels(rng, shape, pieces, -0.22, 0.18)
    return jnp.clip(array, -bound, bound).astype(kind)


def setup_inputs(seed: int = 0) -> dict:
    arg_keys = jax.random.split(jax.random.key(seed), 7)
    return {
        "q_nope": bell_draw(arg_keys[0], (SEQ, HEADS, HEAD_DIM), 1.0, 6.0, ((0, 32), (1, 4))),
        "q_rope": draw_q_rope(jax.random.fold_in(arg_keys[6], 71), 0),
        "latent": draw_latent(jax.random.fold_in(arg_keys[6], 71), 0),
        "up_keys": bell_draw(arg_keys[3], (HEADS, HEAD_DIM, D_LAT), D_LAT ** -0.5, 0.25, ((0, 4),)),
        "up_values": bell_draw(arg_keys[4], (HEADS, D_LAT, HEAD_DIM), 16 ** -0.5, 1.5, ((0, 4),)),
        "out_grad": bell_draw(arg_keys[5], (SEQ, HEADS, HEAD_DIM), 1.0, 6.0, ((0, 32), (1, 4))),
    }


def group_order():
    half_rows = ROWS // 2
    blocks = []
    for block_num in range(2 * N_CTX):
        holder = block_num if block_num < N_CTX else 2 * N_CTX - 1 - block_num
        offset = holder * ROWS + (0 if block_num < N_CTX else half_rows)
        blocks.append(np.arange(offset, offset + half_rows))
    return np.concatenate(blocks).astype(np.int32)


def lowered(values):
    return lax.optimization_barrier(values.astype(jnp.bfloat16)).astype(jnp.float32)


def reference(q_nope, q_rope, latent, up_keys, up_values, out_grad):
    scale_factor = (HEAD_DIM + D_ROPE) ** -0.5
    half_rows = ROWS // 2
    projected = jnp.einsum("shd,hdc->shc", q_nope.astype(jnp.float32), up_keys.astype(jnp.float32))
    absorbed = jnp.concatenate([projected.astype(jnp.bfloat16), q_rope], axis=2)
    grad_lat_out = jnp.einsum("qhv,hcv->qhc", out_grad.astype(jnp.float32), up_values.astype(jnp.float32)).astype(jnp.bfloat16)
    row_order = group_order()
    inverse = np.argsort(row_order).astype(np.int32)
    queries_all = absorbed[row_order].astype(jnp.float32)
    keys_all = latent[row_order].astype(jnp.float32)
    grads_all = grad_lat_out[row_order].astype(jnp.float32)
    triangle = jnp.tril(jnp.ones((half_rows, half_rows), dtype=bool))
    outputs_list = []
    grad_list = []
    grad_latent = jnp.zeros((SEQ, D_LAT + D_ROPE), jnp.float32)
    for block_num in range(2 * N_CTX):
        first_row = block_num * half_rows
        end_row = first_row + half_rows
        queries = queries_all[first_row:end_row]
        key_rows = keys_all[:end_row]
        grads = grads_all[first_row:end_row]
        visible = jnp.concatenate([jnp.ones((half_rows, first_row), dtype=bool), triangle], axis=1)
        scores = jnp.einsum("qhc,kc->hqk", queries, key_rows) * scale_factor
        scores = jnp.where(visible[None], scores, -jnp.inf)
        highest = jnp.max(scores, axis=2, keepdims=True)
        log_total = highest + jnp.log(jnp.sum(jnp.exp(scores - highest), axis=2, keepdims=True))
        probs = jnp.exp(scores - log_total)
        probs_low = lowered(probs)
        lat_out = jnp.einsum("hqk,kc->qhc", probs_low, key_rows[:, :D_LAT])
        dprobs = jnp.einsum("qhc,kc->hqk", grads, key_rows[:, :D_LAT])
        row_delta = jnp.sum(grads * lat_out, axis=2).T
        grad_scores = lowered(probs * (dprobs - row_delta[:, :, None]) * scale_factor)
        grad_list.append(jnp.einsum("hqk,kc->qhc", grad_scores, key_rows))
        value_term = jnp.einsum("hqk,qhc->kc", probs_low, grads)
        latent_term = jnp.einsum("hqk,qhc->kc", grad_scores, queries) + jnp.pad(value_term, ((0, 0), (0, D_ROPE)))
        grad_latent = grad_latent.at[:end_row].add(latent_term)
        outputs_list.append(lat_out)
    lat_out_all = jnp.concatenate(outputs_list, axis=0)[inverse]
    grad_absorbed = jnp.concatenate(grad_list, axis=0)[inverse].astype(jnp.bfloat16)
    attn_out = jnp.einsum("qhc,hcv->qhv", lowered(lat_out_all), up_values.astype(jnp.float32)).astype(jnp.bfloat16)
    grad_q_nope = jnp.einsum("qhc,hdc->qhd", grad_absorbed[:, :, :D_LAT].astype(jnp.float32), up_keys.astype(jnp.float32)).astype(jnp.bfloat16)
    grad_q_rope = grad_absorbed[:, :, D_LAT:]
    return (attn_out, grad_q_nope, grad_q_rope, grad_latent[inverse])
```

```python
import functools, math
import jax, jax.numpy as jnp
from jax import lax
from jax.experimental import pallas as pl
from jax.experimental.pallas import tpu as pltpu
F32, BF16 = jnp.float32, jnp.bfloat16
SCALE = 192 ** -0.5
NEG = -1e30

def dot(a, b):
    return jnp.dot(a, b, preferred_element_type=F32)

def dot_nt(a, b):
    return lax.dot_general(a, b, (((1,), (1,)), ((), ())), preferred_element_type=F32)

def core(t0, lat, q, qr, og, wk, wv, attn, gq, gqr, dl,
         A, AT, G, GT, LT, S, O, DA, m, l, lse, delta, dsb, pbb, acc):
    log2k = SCALE * math.log2(math.e)
    c_dyn = t0[0]
    tt = t0[1]
    @pl.loop(0, 8)
    def _(p):
        lanes = pl.ds(pl.multiple_of(p * 128, 128), 128)
        pa = dot(q[2 * p], wk[2 * p])
        pb = dot(q[2 * p + 1], wk[2 * p + 1])
        ga = dot_nt(og[2 * p], wv[2 * p])
        gb = dot_nt(og[2 * p + 1], wv[2 * p + 1])
        ra, rb = qr[2 * p], qr[2 * p + 1]
        for hf in range(2):
            r = slice(64 * hf, 64 * hf + 64)
            blk = jnp.concatenate([pa[r], pb[r]], axis=0)
            A[hf, lanes, :512] = blk.astype(BF16)
            AT[hf, :512, lanes] = blk.T.astype(BF16)
            rblk = jnp.concatenate([ra[r], rb[r]], axis=0)
            A[hf, lanes, 512:] = rblk
            AT[hf, 512:, lanes] = rblk.astype(F32).T.astype(BF16)
            gblk = jnp.concatenate([ga[r], gb[r]], axis=0)
            G[hf, lanes, :] = gblk.astype(BF16)
            GT[hf, :, lanes] = gblk.T.astype(BF16)
    m[...] = jnp.full_like(m, NEG)
    l[...] = jnp.zeros_like(l)
    O[...] = jnp.zeros_like(O)
    DA[...] = jnp.zeros_like(DA)
    c = c_dyn

    def fwd(t, hf):
        slot = jnp.where(hf == 1, t, 16 - t)
        base = jnp.where(hf == 1, 63 - c, c) * 64 - t * 256
        Lt = lat[pl.ds(pl.multiple_of(t * 256, 256), 256), :]
        diff = lax.broadcasted_iota(jnp.int32, (256, 256), 0) - lax.rem(lax.broadcasted_iota(jnp.int32, (256, 256), 1), 64)
        for ch in range(4):
            cs = slice(ch * 256, ch * 256 + 256)
            s = dot(Lt, AT[hf, :, cs]) * log2k
            S[slot, :, cs] = jnp.where(diff <= base, s, NEG)
        als = []
        for ch in range(4):
            cs = slice(ch * 256, ch * 256 + 256)
            s = S[slot, :, cs]
            mo = m[hf, :, cs]
            mn = jnp.maximum(mo, jnp.max(s, axis=0, keepdims=True))
            p = jnp.exp2(s - mn)
            al = jnp.exp2(mo - mn)
            m[hf, :, cs] = mn
            l[hf, :, cs] = l[hf, :, cs] * al + jnp.sum(p, axis=0, keepdims=True)
            pbb[:, cs] = p.astype(BF16)
            als.append(al)
        for ch in range(4):
            cs = slice(ch * 256, ch * 256 + 256)
            O[hf, :, cs] = O[hf, :, cs] * als[ch] + dot(LT[t, :512, :], pbb[:, cs])

    @pl.loop(0, 16)
    def _(t):
        LT[t] = lat[pl.ds(pl.multiple_of(t * 256, 256), 256), :].astype(F32).T.astype(BF16)
        @pl.when(t <= 15 - tt)
        def _():
            fwd(t, 1)
        @pl.when(t <= tt)
        def _():
            fwd(t, 0)
    for hf in range(2):
        for ch in range(4):
            cs = slice(ch * 256, ch * 256 + 256)
            lse[hf, :, cs] = m[hf, :, cs] + jnp.log2(l[hf, :, cs])
            o = O[hf, :, cs] * (1.0 / l[hf, :, cs])
            O[hf, :, cs] = o
            delta[hf, :, cs] = jnp.sum(GT[hf, :, cs].astype(F32) * o, axis=0, keepdims=True)

    def bwd(t, hf):
        slot = jnp.where(hf == 1, t, 16 - t)
        Lt = lat[pl.ds(pl.multiple_of(t * 256, 256), 256), :512]
        for ch in range(4):
            cs = slice(ch * 256, ch * 256 + 256)
            dp = dot(Lt, GT[hf, :, cs])
            p = jnp.exp2(S[slot, :, cs] - lse[hf, :, cs])
            ds = (p * (dp - delta[hf, :, cs]) * SCALE).astype(BF16)
            dsb[:, cs] = ds
            pbb[:, cs] = p.astype(BF16)
            DA[hf, :, cs] += dot(LT[t], ds)
        return dot(dsb[...], A[hf]), dot(pbb[...], G[hf])

    @pl.loop(0, 16)
    def _(t):
        rows = pl.ds(pl.multiple_of(t * 256, 256), 256)
        @pl.when(t <= 15 - tt)
        def _():
            a, b = bwd(t, 1)
            acc[:, :512] = a[:, :512] + b
            acc[:, 512:] = a[:, 512:]
        @pl.when(t > 15 - tt)
        def _():
            acc[...] = jnp.zeros((256, 576), F32)
        @pl.when(t <= tt)
        def _():
            a, b = bwd(t, 0)
            acc[:, :512] += a[:, :512] + b
            acc[:, 512:] += a[:, 512:]
        dl[rows, :] = acc[...].astype(BF16)
    @pl.loop(0, 8)
    def _(p):
        lanes = pl.ds(pl.multiple_of(p * 128, 128), 128)
        ob = [O[hf, :, lanes].T.astype(BF16) for hf in range(2)]
        db = [DA[hf, :, lanes].T.astype(BF16) for hf in range(2)]
        for e in range(2):
            r = slice(64 * e, 64 * e + 64)
            h = 2 * p + e
            o = jnp.concatenate([ob[0][r], ob[1][r]], axis=0)
            d = jnp.concatenate([db[0][r], db[1][r]], axis=0)
            attn[h] = dot(o, wv[h]).astype(BF16)
            gq[h] = dot_nt(d[:, :512], wk[h]).astype(BF16)
            gqr[h] = d[:, 512:]

SCR = [
    pltpu.VMEM((2, 1024, 576), BF16), pltpu.VMEM((2, 576, 1024), BF16),
    pltpu.VMEM((2, 1024, 512), BF16), pltpu.VMEM((2, 512, 1024), BF16),
    pltpu.VMEM((16, 576, 256), BF16), pltpu.VMEM((17, 256, 1024), F32),
    pltpu.VMEM((2, 512, 1024), F32), pltpu.VMEM((2, 576, 1024), F32),
    pltpu.VMEM((2, 1, 1024), F32), pltpu.VMEM((2, 1, 1024), F32), pltpu.VMEM((2, 1, 1024), F32), pltpu.VMEM((2, 1, 1024), F32),
    pltpu.VMEM((256, 1024), BF16), pltpu.VMEM((256, 1024), BF16), pltpu.VMEM((256, 576), F32),
]
def call():
    V = pl.BlockSpec(memory_space=pltpu.VMEM)
    return pl.pallas_call(core,
        out_shape=[jax.ShapeDtypeStruct((16, 128, 128), BF16), jax.ShapeDtypeStruct((16, 128, 128), BF16),
                   jax.ShapeDtypeStruct((16, 128, 64), BF16), jax.ShapeDtypeStruct((4096, 576), BF16)],
        in_specs=[pl.BlockSpec(memory_space=pltpu.SMEM)] + [V] * 6,
        out_specs=[V] * 4, scratch_shapes=SCR,
        compiler_params=pltpu.CompilerParams(vmem_limit_bytes=63 * 2**20))


def body(q_nope, q_rope, latent, up_keys, up_values, out_grad):
    c = lax.axis_index("ctx")
    info = jnp.stack([c, c // 4]).astype(jnp.int32)
    full = lax.all_gather(latent, "ctx", axis=0, tiled=True).reshape(32, 2, 64, 576)
    keys = jnp.concatenate([full[:, 0], full[::-1, 1]], axis=0).reshape(4096, 576)
    heads = lambda z: jnp.swapaxes(z, 0, 1)
    attn, gq, gqr, dl = call()(info, keys, heads(q_nope), heads(q_rope), heads(out_grad), up_keys, up_values)
    dl = dl.reshape(2, 32, 64, 576)
    dl = jnp.stack([dl[0], dl[1, ::-1]], axis=1).reshape(4096, 576)
    part = lax.psum_scatter(dl, "ctx", scatter_dimension=0, tiled=True)
    return heads(attn), heads(gq), heads(gqr), lax.psum(part, "tp").astype(F32)


def solution(mesh):
    from jax.sharding import PartitionSpec as P
    rows = P("ctx", "tp", None)
    return jax.shard_map(
        body, mesh=mesh,
        in_specs=(rows, rows, P("ctx", None), P("tp", None, None), P("tp", None, None), rows),
        out_specs=(rows, rows, rows, P("ctx", None)), check_vma=False)
```

```python
import math

import jax
import jax.numpy as jnp
from jax import lax
from jax.experimental import pallas as pl
from jax.experimental.pallas import tpu as pltpu
from jax.sharding import PartitionSpec as P

F32, BF16 = jnp.float32, jnp.bfloat16
SCALE = 192**-0.5
LOG2_SCALE = SCALE * math.log2(math.e)
NEG = -1e30
MESH = pl.DeviceIdType.MESH


def dot(a, b):
    return jnp.dot(a, b, preferred_element_type=F32)


def dot_nt(a, b):
    return lax.dot_general(a, b, (((1,), (1,)), ((), ())), preferred_element_type=F32)


def remote(src, dst, send_sem, recv_sem, ctx, tp):
    return pltpu.make_async_remote_copy(
        src_ref=src, dst_ref=dst, send_sem=send_sem, recv_sem=recv_sem,
        device_id={"ctx": ctx, "tp": tp}, device_id_type=MESH,
    )


def kernel(lat, q, qr, og, wk, wv, attn, gq, gqr, gl,
           L, LT, A, AT, G, GT, S, O, DA, top, tot, lse, delta, dsb, pbb, acc,
           R1, R2, R3s, R3, fin,
           sx, rx, sz, rz, sy, ry, ss, rs, s1, r1, s2, r2, s3, r3, s4, r4):
    c, tp = lax.axis_index("ctx"), lax.axis_index("tp")
    z, yl, x = c // 8, (c // 4) % 2, c % 4
    yh, k = tp // 2, tp % 2
    t0 = c // 4
    sib = yh * 2 + 1 - k

    def cid(z_, yl_, x_):
        return z_ * 8 + yl_ * 4 + x_

    def tile_of(kind, line):
        return jnp.where(kind == 0, line, 15 - line)

    def block_at(x_):
        return pl.multiple_of(64 * jnp.where(k == 0, x_, 3 - x_), 64)

    def order(s):
        i = s % 4
        return i + jnp.where(i == 2, 1, 0) - jnp.where(i == 3, 1, 0), s // 4

    def line_at(dz, dy):
        return 2 * ((z + dz) % 4) + (yl + dy) % 2

    def active(kind, line):
        return (kind == 0) | (line >= t0)

    barrier = pltpu.get_barrier_semaphore()

    def hello(ctx, tp_):
        pl.semaphore_signal(barrier, inc=1, device_id={"ctx": ctx, "tp": tp_}, device_id_type=MESH)

    @pl.loop(1, 4)
    def _(i):
        hello(cid(z, yl, (x + i) % 4), tp)

    @pl.loop(1, 16)
    def _(i):
        hello(cid((z + i // 4) % 4, (yl + (i // 2) % 2) % 2, x), ((yh + i % 2) % 2) * 2 + k)

    hello(c, sib)
    hello(c, (1 - yh) * 2 + 1 - k)
    pl.semaphore_wait(barrier, 20)

    mine = tile_of(k, t0)

    def x_copy(dx):
        at = L.at[mine, pl.ds(block_at(x), 64), :]
        return remote(at, at, sx.at[dx - 1], rx.at[dx - 1], cid(z, yl, (x + dx) % 4), tp)

    def z_copy(dz):
        at = L.at[mine]
        return remote(at, at, sz.at[dz - 1], rz.at[3 - dz], cid((z + dz) % 4, yl, x), tp)

    def y_copy(dz, to):
        at = L.at[tile_of(k, line_at(dz, 0)), pl.ds(pl.multiple_of(128 * yh, 128), 128), :]
        return remote(at, at, sy.at[dz, to], ry.at[dz, yh], cid(z, 1 - yl, x), to * 2 + k)

    def core_copy(s, line):
        at = L.at[tile_of(k, line)]
        return remote(at, at, ss.at[s], rs.at[s], c, sib)

    L[mine, pl.ds(block_at(x), 64), :] = lat[pl.ds(pl.multiple_of(64 * k, 64), 64), :]
    for dx in (1, 3, 2):
        x_copy(dx).start()

    @pl.loop(0, 8)
    def _(p):
        cols = pl.ds(pl.multiple_of(p * 128, 128), 128)
        pa = dot(q[2 * p], wk[2 * p])
        pb = dot(q[2 * p + 1], wk[2 * p + 1])
        ga = dot_nt(og[2 * p], wv[2 * p])
        gb = dot_nt(og[2 * p + 1], wv[2 * p + 1])
        ra, rb = qr[2 * p], qr[2 * p + 1]
        for hf in range(2):
            r = slice(64 * hf, 64 * hf + 64)
            blk = jnp.concatenate([pa[r], pb[r]], axis=0)
            A[hf, cols, :512] = blk.astype(BF16)
            AT[hf, :512, cols] = blk.T.astype(BF16)
            rblk = jnp.concatenate([ra[r], rb[r]], axis=0)
            A[hf, cols, 512:] = rblk
            AT[hf, 512:, cols] = rblk.astype(F32).T.astype(BF16)
            gblk = jnp.concatenate([ga[r], gb[r]], axis=0)
            G[hf, cols, :] = gblk.astype(BF16)
            GT[hf, :, cols] = gblk.T.astype(BF16)

    top[...] = jnp.full_like(top, NEG)
    tot[...] = jnp.zeros_like(tot)
    O[...] = jnp.zeros_like(O)
    DA[...] = jnp.zeros_like(DA)

    def slot_of(t, hf):
        return jnp.where(hf == 1, t, 16 - t)

    def forward(t, hf):
        slot = slot_of(t, hf)
        base = jnp.where(hf == 1, 63 - c, c) * 64 - t * 256
        diff = lax.broadcasted_iota(jnp.int32, (256, 256), 0) - lax.rem(
            lax.broadcasted_iota(jnp.int32, (256, 256), 1), 64)
        for ch in range(4):
            cs = slice(ch * 256, ch * 256 + 256)
            s = dot(L[t], AT[hf, :, cs]) * LOG2_SCALE
            S[slot, :, cs] = jnp.where(diff <= base, s, NEG)
        shrink = []
        for ch in range(4):
            cs = slice(ch * 256, ch * 256 + 256)
            s = S[slot, :, cs]
            old = top[hf, :, cs]
            new = jnp.maximum(old, jnp.max(s, axis=0, keepdims=True))
            p = jnp.exp2(s - new)
            al = jnp.exp2(old - new)
            top[hf, :, cs] = new
            tot[hf, :, cs] = tot[hf, :, cs] * al + jnp.sum(p, axis=0, keepdims=True)
            pbb[:, cs] = p.astype(BF16)
            shrink.append(al)
        for ch in range(4):
            cs = slice(ch * 256, ch * 256 + 256)
            O[hf, :, cs] = O[hf, :, cs] * shrink[ch] + dot(LT[t, :512, :], pbb[:, cs])

    for dx in (1, 2, 3):
        x_copy(dx).wait_recv()
    for dz in (1, 3, 2):
        z_copy(dz).start()

    @pl.loop(0, 8)
    def _(s):
        dz, dy = order(s)
        line = line_at(dz, dy)

        @pl.when((dy == 0) & (dz > 0))
        def _():
            z_copy(4 - dz).wait_recv()

        @pl.when(dy == 0)
        def _():
            for to in range(2):
                y_copy(dz, to).start()

        @pl.when(dy == 1)
        def _():
            for frm in range(2):
                at = L.at[tile_of(k, line), 128 * frm:128 * frm + 128, :]
                remote(at, at, sy.at[dz, 0], ry.at[dz, frm], cid(z, 1 - yl, x), frm * 2 + k).wait_recv()

        core_copy(s, line).start()

        @pl.loop(0, 2)
        def _(kk):
            @pl.when(kk == 1)
            def _():
                at = L.at[tile_of(1 - k, line)]
                remote(at, at, ss.at[s], rs.at[s], c, sib).wait_recv()

            t = tile_of((k + kk) % 2, line)

            @pl.when(t <= 15 - t0)
            def _():
                LT[t] = L[t].astype(F32).T.astype(BF16)

            @pl.loop(0, 2)
            def _(i):
                @pl.when(((i == 0) & (t <= 15 - t0)) | ((i == 1) & (t <= t0)))
                def _():
                    forward(t, 1 - i)

    for hf in range(2):
        for ch in range(4):
            cs = slice(ch * 256, ch * 256 + 256)
            lse[hf, :, cs] = top[hf, :, cs] + jnp.log2(tot[hf, :, cs])
            o = O[hf, :, cs] * (1.0 / tot[hf, :, cs])
            O[hf, :, cs] = o
            delta[hf, :, cs] = jnp.sum(GT[hf, :, cs].astype(F32) * o, axis=0, keepdims=True)

    for d in (1, 2, 3):
        x_copy(d).wait_send()
        z_copy(d).wait_send()

    @pl.loop(0, 8)
    def _(s):
        dz, dy = order(s)

        @pl.when(dy == 0)
        def _():
            for to in range(2):
                y_copy(dz, to).wait_send()

        core_copy(s, line_at(dz, dy)).wait_send()

    def backward(t, hf):
        slot = slot_of(t, hf)
        for ch in range(4):
            cs = slice(ch * 256, ch * 256 + 256)
            dp = dot(L[t, :, :512], GT[hf, :, cs])
            p = jnp.exp2(S[slot, :, cs] - lse[hf, :, cs])
            dsb[:, cs] = (p * (dp - delta[hf, :, cs]) * SCALE).astype(BF16)
            pbb[:, cs] = p.astype(BF16)
        for ch in range(4):
            cs = slice(ch * 256, ch * 256 + 256)
            DA[hf, :, cs] += dot(LT[t], dsb[:, cs])
        a, b = dot(dsb[...], A[hf]), dot(pbb[...], G[hf])
        acc[:, :512] += a[:, :512] + b
        acc[:, 512:] += a[:, 512:]

    def r1_copy(s, line):
        return remote(L.at[tile_of(1 - k, line)], R1.at[s], s1.at[s], r1.at[s], c, sib)

    def r2_copy(s, line, dx):
        to = (x + dx) % 4
        return remote(L.at[tile_of(k, line), pl.ds(block_at(to), 64), :], R2.at[s, dx - 1],
                      s2.at[s, dx - 1], r2.at[s, dx - 1], cid(z, yl, to), tp)

    def r3_copy(s, to):
        dz, dy = order(s)
        slot = ((4 - dz) % 4) * 4 + dy * 2 + (yh + to) % 2
        return remote(R3s.at[s, 32 * to:32 * to + 32, :], R3.at[slot], s3.at[s, to], r3.at[slot],
                      cid((z + dz) % 4, (yl + dy) % 2, x), to * 2 + k)

    def finish(s):
        dz, dy = order(s)
        line = line_at(dz, dy)

        @pl.when(active(k, line))
        def _():
            for dx in (1, 2, 3):
                r2_copy(s, line, dx).wait_recv()
            total = L[tile_of(k, line), pl.ds(block_at(x), 64), :].astype(F32)
            for dx in range(3):
                total = total + R2[s, dx].astype(F32)
            R3s[s] = total.astype(BF16)
            for to in range(2):
                @pl.when((s > 0) | (yh != to))
                def _():
                    r3_copy(s, to).start()

                @pl.when((s == 0) & (yh == to))
                def _():
                    R3[0] = R3s[0, 32 * to:32 * to + 32, :]

    @pl.loop(0, 8)
    def _(i):
        s = 7 - i
        dz, dy = order(s)
        line = line_at(dz, dy)

        @pl.loop(0, 2)
        def _(kk):
            kind = (k + 1 - kk) % 2
            t = tile_of(kind, line)

            @pl.when((kk == 1) & (s < 7))
            def _():
                finish(s + 1)

            @pl.when(active(kind, line))
            def _():
                acc[...] = jnp.zeros_like(acc)

                @pl.loop(0, 2)
                def _(i):
                    @pl.when((i == 0) | (t <= t0))
                    def _():
                        backward(t, 1 - i)

                @pl.when(kk == 0)
                def _():
                    L[t] = acc[...].astype(BF16)
                    r1_copy(s, line).start()

                @pl.when(kk == 1)
                def _():
                    remote(L.at[t], R1.at[s], s1.at[s], r1.at[s], c, sib).wait_recv()
                    L[t] = (acc[...] + R1[s].astype(F32)).astype(BF16)
                    for dx in (1, 3, 2):
                        r2_copy(s, line, dx).start()

    @pl.loop(0, 8)
    def _(p):
        cols = pl.ds(pl.multiple_of(p * 128, 128), 128)
        ob = [O[hf, :, cols].T.astype(BF16) for hf in range(2)]
        db = [DA[hf, :, cols].T.astype(BF16) for hf in range(2)]
        for e in range(2):
            r = slice(64 * e, 64 * e + 64)
            h = 2 * p + e
            o = jnp.concatenate([ob[0][r], ob[1][r]], axis=0)
            d = jnp.concatenate([db[0][r], db[1][r]], axis=0)
            attn[h] = dot(o, wv[h]).astype(BF16)
            gq[h] = dot_nt(d[:, :512], wk[h]).astype(BF16)
            gqr[h] = d[:, 512:]

        @pl.when(p == 0)
        def _():
            finish(0)

    my_rows = pl.ds(pl.multiple_of(64 * k + 32 * yh, 32), 32)
    fin[my_rows, :] = R3[0].astype(F32)

    @pl.loop(1, 16)
    def _(slot):
        source = 2 * ((z + slot // 4) % 4) + (yl + (slot // 2) % 2) % 2

        @pl.when((k == 0) | (t0 >= source))
        def _():
            at = R3.at[slot]
            remote(at, at, s3.at[0, 0], r3.at[slot], c, sib).wait_recv()
            fin[my_rows, :] += at[...].astype(F32)

    def r4_copy(j):
        at = fin.at[my_rows, :]
        return remote(at, at, s4.at[j - 1], r4.at[j - 1], c, ((yh + j // 2) % 2) * 2 + (k + j % 2) % 2)

    for j in (1, 2, 3):
        r4_copy(j).start()

    @pl.loop(0, 8)
    def _(s):
        dz, dy = order(s)
        line = line_at(dz, dy)

        @pl.when(active(1 - k, line))
        def _():
            r1_copy(s, line).wait_send()

        @pl.when(active(k, line))
        def _():
            for dx in (1, 2, 3):
                r2_copy(s, line, dx).wait_send()
            for to in range(2):
                @pl.when((s > 0) | (yh != to))
                def _():
                    r3_copy(s, to).wait_send()

    for j in (1, 2, 3):
        r4_copy(j).wait()
    gl[...] = fin[...]


DMA = pltpu.SemaphoreType.DMA
SCRATCH = [
    pltpu.VMEM((16, 256, 576), BF16),
    pltpu.VMEM((16, 576, 256), BF16),
    pltpu.VMEM((2, 1024, 576), BF16),
    pltpu.VMEM((2, 576, 1024), BF16),
    pltpu.VMEM((2, 1024, 512), BF16),
    pltpu.VMEM((2, 512, 1024), BF16),
    pltpu.VMEM((17, 256, 1024), F32),
    pltpu.VMEM((2, 512, 1024), F32),
    pltpu.VMEM((2, 576, 1024), F32),
    pltpu.VMEM((2, 1, 1024), F32),
    pltpu.VMEM((2, 1, 1024), F32),
    pltpu.VMEM((2, 1, 1024), F32),
    pltpu.VMEM((2, 1, 1024), F32),
    pltpu.VMEM((256, 1024), BF16),
    pltpu.VMEM((256, 1024), BF16),
    pltpu.VMEM((256, 576), F32),
    pltpu.VMEM((8, 256, 576), BF16),
    pltpu.VMEM((8, 3, 64, 576), BF16),
    pltpu.VMEM((8, 64, 576), BF16),
    pltpu.VMEM((16, 32, 576), BF16),
    pltpu.VMEM((128, 576), F32),
    DMA((3,)), DMA((3,)), DMA((3,)), DMA((3,)), DMA((4, 2)), DMA((4, 2)), DMA((8,)), DMA((8,)),
    DMA((8,)), DMA((8,)), DMA((8, 3)), DMA((8, 3)), DMA((8, 2)), DMA((16,)), DMA((3,)), DMA((3,)),
]


def body(q_nope, q_rope, latent, up_keys, up_values, out_grad):
    def heads(v):
        return jnp.swapaxes(v, 0, 1)

    vmem = pl.BlockSpec(memory_space=pltpu.VMEM)
    attn, gq, gqr, gl = pl.pallas_call(
        kernel,
        out_shape=[
            jax.ShapeDtypeStruct((16, 128, 128), BF16),
            jax.ShapeDtypeStruct((16, 128, 128), BF16),
            jax.ShapeDtypeStruct((16, 128, 64), BF16),
            jax.ShapeDtypeStruct((128, 576), F32),
        ],
        in_specs=[vmem] * 6,
        out_specs=[vmem] * 4,
        scratch_shapes=SCRATCH,
        compiler_params=pltpu.CompilerParams(
            vmem_limit_bytes=63 * 2**20, collective_id=0, has_side_effects=True),
        cost_estimate=pl.CostEstimate(flops=30_000_000_000, bytes_accessed=12_000_000, transcendentals=9_000_000),
    )(latent, heads(q_nope), heads(q_rope), heads(out_grad), up_keys, up_values)
    return heads(attn), heads(gq), heads(gqr), gl


def solution(mesh):
    rows = P("ctx", "tp", None)
    return jax.shard_map(
        body, mesh=mesh,
        in_specs=(rows, rows, P("ctx", None), P("tp", None, None), P("tp", None, None), rows),
        out_specs=(rows, rows, rows, P("ctx", None)),
        check_vma=False,
    )
```

```python
import math

import jax
import jax.numpy as jnp
from jax import lax
from jax.experimental import pallas as pl
from jax.experimental.pallas import tpu as pltpu
from jax.sharding import PartitionSpec as P

F32, BF16 = jnp.float32, jnp.bfloat16
SCALE = 192**-0.5
LOG2_SCALE = SCALE * math.log2(math.e)
NEG = -1e30
MESH = pl.DeviceIdType.MESH


def dot(a, b):
    return jnp.dot(a, b, preferred_element_type=F32)


def dot_nt(a, b):
    return lax.dot_general(a, b, (((1,), (1,)), ((), ())), preferred_element_type=F32)


def remote(src, dst, send_sem, recv_sem, ctx, tp):
    return pltpu.make_async_remote_copy(
        src_ref=src, dst_ref=dst, send_sem=send_sem, recv_sem=recv_sem,
        device_id={"ctx": ctx, "tp": tp}, device_id_type=MESH,
    )


def kernel(lat_hbm, q_hbm, qr_hbm, og_hbm, wk_hbm, wv_hbm, attn_hbm, gq_hbm, gqr_hbm, gl_hbm,
           lat, q, qr, og, wk, wv, X, sin, sout,
           L, LT, A, AT, G, GT, S, O, DA, top, tot, lse, delta, dsb, pbb, acc,
           R1, R2, R3s, R3, fin, flip,
           sx, rx, sz, rz, sb, rb, sy, ry, ss, rs, s1, r1, s2, r2, s3, r3, s4, r4):
    c, tp = lax.axis_index("ctx"), lax.axis_index("tp")
    z, yl, x = c // 8, (c // 4) % 2, c % 4
    yh, k = tp // 2, tp % 2
    t0 = c // 4
    sib = yh * 2 + 1 - k

    def cid(z_, yl_, x_):
        return z_ * 8 + yl_ * 4 + x_

    def tile_of(kind, line):
        return jnp.where(kind == 0, line, 15 - line)

    def block_at(x_):
        return pl.multiple_of(64 * jnp.where(k == 0, x_, 3 - x_), 64)

    def order(s):
        i = jnp.where(s >= 5, s - 4, s - 1)
        dz = i + jnp.where(i == 2, 1, 0) - jnp.where(i == 3, 1, 0)
        return jnp.where(s <= 1, 0, dz), jnp.where((s == 1) | (s >= 5), 1, 0)

    def line_at(dz, dy):
        return 2 * ((z + dz) % 4) + (yl + dy) % 2

    def active(kind, line):
        return (kind == 0) | (line >= t0)

    mine = tile_of(k, t0)
    loads = [
        pltpu.make_async_copy(src, dst, sin.at[i]) for i, (src, dst) in enumerate((
            (lat_hbm, lat),
            (q_hbm, q), (wk_hbm, wk), (qr_hbm, qr), (og_hbm, og), (wv_hbm, wv)))
    ]
    for load in loads:
        load.start()

    barrier = pltpu.get_barrier_semaphore()

    def hello(ctx, tp_):
        pl.semaphore_signal(barrier, inc=1, device_id={"ctx": ctx, "tp": tp_}, device_id_type=MESH)

    @pl.loop(1, 4)
    def _(i):
        hello(cid(z, yl, (x + i) % 4), tp)

    @pl.loop(1, 16)
    def _(i):
        hello(cid((z + i // 4) % 4, (yl + (i // 2) % 2) % 2, x), ((yh + i % 2) % 2) * 2 + k)

    hello(c, sib)
    hello(c, (1 - yh) * 2 + 1 - k)
    pl.semaphore_wait(barrier, 20)

    def x_copy(dx):
        at = L.at[mine, pl.ds(block_at(x), 64), :]
        return remote(at, at, sx.at[dx - 1], rx.at[dx - 1], cid(z, yl, (x + dx) % 4), tp)

    def z_copy(dz):
        at = L.at[mine]
        return remote(at, at, sz.at[dz - 1], rz.at[3 - dz], cid((z + dz) % 4, yl, x), tp)

    def zb_copy(dz):
        at = L.at[mine, pl.ds(block_at(x), 64), :]
        return remote(at, at, sz.at[dz - 1], rz.at[3 - dz], cid((z + dz) % 4, yl, x), tp)

    def xb_copy(dz, dx):
        at = L.at[tile_of(k, line_at(dz, 0)), pl.ds(block_at(x), 64), :]
        return remote(at, at, sb.at[dz - 1, dx - 1], rb.at[dz - 1, dx - 1], cid(z, yl, (x + dx) % 4), tp)

    def wait_line(dz):
        @pl.when(k == 0)
        def _():
            z_copy(4 - dz).wait_recv()

        @pl.when(k == 1)
        def _():
            for dx in (1, 3, 2):
                xb_copy(dz, dx).wait_recv()

    def y_copy(dz, to):
        at = L.at[tile_of(k, line_at(dz, 0)), pl.ds(pl.multiple_of(128 * yh, 128), 128), :]
        return remote(at, at, sy.at[dz, to], ry.at[dz, yh], cid(z, 1 - yl, x), to * 2 + k)

    def core_copy(s, line):
        at = L.at[tile_of(k, line)]
        return remote(at, at, ss.at[s], rs.at[s], c, sib)

    loads[0].wait()
    fin[...] = lat[...].astype(F32).T
    L[mine, pl.ds(block_at(x), 64), :] = fin[pl.ds(pl.multiple_of(64 * k, 64), 64), :].astype(BF16)
    for dx in (1, 3, 2):
        x_copy(dx).start()

    @pl.when(k == 1)
    def _():
        for dz in (1, 3, 2):
            zb_copy(dz).start()

    for load in loads[1:]:
        load.wait()
    X[0] = q[...].astype(F32)
    X[1] = og[...].astype(F32)

    def head(i, h):
        return X[i, pl.ds(h, 128, stride=16), :]

    @pl.loop(0, 8)
    def _(p):
        cols = pl.ds(pl.multiple_of(p * 128, 128), 128)
        pa = dot(head(0, 2 * p).astype(BF16), wk[2 * p])
        pb = dot(head(0, 2 * p + 1).astype(BF16), wk[2 * p + 1])
        ga = dot_nt(head(1, 2 * p).astype(BF16), wv[2 * p])
        gb = dot_nt(head(1, 2 * p + 1).astype(BF16), wv[2 * p + 1])
        ra, rb = qr[2 * p].astype(F32).T, qr[2 * p + 1].astype(F32).T
        for hf in range(2):
            r = slice(64 * hf, 64 * hf + 64)
            blk = jnp.concatenate([pa[r], pb[r]], axis=0)
            A[hf, cols, :512] = blk.astype(BF16)
            AT[hf, :512, cols] = blk.T.astype(BF16)
            rblk = jnp.concatenate([ra[r], rb[r]], axis=0)
            A[hf, cols, 512:] = rblk.astype(BF16)
            AT[hf, 512:, cols] = rblk.T.astype(BF16)
            gblk = jnp.concatenate([ga[r], gb[r]], axis=0)
            G[hf, cols, :] = gblk.astype(BF16)
            GT[hf, :, cols] = gblk.T.astype(BF16)

    top[...] = jnp.full_like(top, NEG)
    tot[...] = jnp.zeros_like(tot)
    O[...] = jnp.zeros_like(O)
    DA[...] = jnp.zeros_like(DA)

    def slot_of(t, hf):
        return jnp.where(hf == 1, t, 16 - t)

    def forward(t, hf):
        slot = slot_of(t, hf)
        base = jnp.where(hf == 1, 63 - c, c) * 64 - t * 256
        diff = lax.broadcasted_iota(jnp.int32, (256, 256), 0) - lax.rem(
            lax.broadcasted_iota(jnp.int32, (256, 256), 1), 64)
        for ch in range(4):
            cs = slice(ch * 256, ch * 256 + 256)
            s = dot(L[t], AT[hf, :, cs]) * LOG2_SCALE
            S[slot, :, cs] = jnp.where(diff <= base, s, NEG)
        shrink = []
        for ch in range(4):
            cs = slice(ch * 256, ch * 256 + 256)
            s = S[slot, :, cs]
            old = top[hf, :, cs]
            new = jnp.maximum(old, jnp.max(s, axis=0, keepdims=True))
            p = jnp.exp2(s - new)
            al = jnp.exp2(old - new)
            top[hf, :, cs] = new
            tot[hf, :, cs] = tot[hf, :, cs] * al + jnp.sum(p, axis=0, keepdims=True)
            pbb[:, cs] = p.astype(BF16)
            shrink.append(al)
        for ch in range(4):
            cs = slice(ch * 256, ch * 256 + 256)
            O[hf, :, cs] = O[hf, :, cs] * shrink[ch] + dot(LT[t, :512, :], pbb[:, cs])

    for dx in (1, 2, 3):
        x_copy(dx).wait_recv()
    @pl.when(k == 0)
    def _():
        for dz in (1, 3):
            z_copy(dz).start()

    def pass_on(s, dz):
        for to in range(2):
            y_copy(dz, to).start()
        core_copy(s, line_at(dz, 0)).start()

    pass_on(0, 0)

    @pl.when(k == 1)
    def _():
        for dz in (1, 3, 2):
            zb_copy(4 - dz).wait_recv()
            for dx in (1, 3, 2):
                xb_copy(dz, dx).start()

    @pl.loop(0, 8)
    def _(s):
        dz, dy = order(s)
        line = line_at(dz, dy)

        @pl.when((s == 1) & (k == 0))
        def _():
            z_copy(2).start()

        @pl.when(s == 2)
        def _():
            for at, dz_ in ((2, 1), (3, 3)):
                wait_line(dz_)
                pass_on(at, dz_)

        @pl.when(s == 4)
        def _():
            wait_line(2)
            pass_on(4, 2)

        @pl.when(dy == 1)
        def _():
            for frm in range(2):
                at = L.at[tile_of(k, line), 128 * frm:128 * frm + 128, :]
                remote(at, at, sy.at[dz, 0], ry.at[dz, frm], cid(z, 1 - yl, x), frm * 2 + k).wait_recv()
            core_copy(s, line).start()

        @pl.loop(0, 2)
        def _(kk):
            @pl.when(kk == 1)
            def _():
                at = L.at[tile_of(1 - k, line)]
                remote(at, at, ss.at[s], rs.at[s], c, sib).wait_recv()

            t = tile_of((k + kk) % 2, line)

            @pl.when(t <= 15 - t0)
            def _():
                LT[t] = L[t].astype(F32).T.astype(BF16)

            @pl.loop(0, 2)
            def _(i):
                @pl.when(((i == 0) & (t <= 15 - t0)) | ((i == 1) & (t <= t0)))
                def _():
                    forward(t, 1 - i)

    for hf in range(2):
        for ch in range(4):
            cs = slice(ch * 256, ch * 256 + 256)
            lse[hf, :, cs] = top[hf, :, cs] + jnp.log2(tot[hf, :, cs])
            o = O[hf, :, cs] * (1.0 / tot[hf, :, cs])
            O[hf, :, cs] = o
            delta[hf, :, cs] = jnp.sum(GT[hf, :, cs].astype(F32) * o, axis=0, keepdims=True)

    for d in (1, 2, 3):
        x_copy(d).wait_send()

        @pl.when(k == 0)
        def _():
            z_copy(d).wait_send()

        @pl.when(k == 1)
        def _():
            zb_copy(d).wait_send()
            for dx in (1, 2, 3):
                xb_copy(d, dx).wait_send()

    @pl.loop(0, 8)
    def _(s):
        dz, dy = order(s)

        @pl.when(dy == 0)
        def _():
            for to in range(2):
                y_copy(dz, to).wait_send()

        core_copy(s, line_at(dz, dy)).wait_send()

    def backward(t, hf):
        slot = slot_of(t, hf)
        for ch in range(4):
            cs = slice(ch * 256, ch * 256 + 256)
            dp = dot(L[t, :, :512], GT[hf, :, cs])
            p = jnp.exp2(S[slot, :, cs] - lse[hf, :, cs])
            dsb[:, cs] = (p * (dp - delta[hf, :, cs]) * SCALE).astype(BF16)
            pbb[:, cs] = p.astype(BF16)
        for ch in range(4):
            cs = slice(ch * 256, ch * 256 + 256)
            DA[hf, :, cs] += dot(LT[t], dsb[:, cs])
        a, b = dot(dsb[...], A[hf]), dot(pbb[...], G[hf])
        acc[:, :512] += a[:, :512] + b
        acc[:, 512:] += a[:, 512:]

    def r1_copy(s, line):
        return remote(L.at[tile_of(1 - k, line)], R1.at[s], s1.at[s], r1.at[s], c, sib)

    def r2x_copy(s, line, dx):
        to = (x + dx) % 4
        return remote(L.at[tile_of(k, line), pl.ds(block_at(to), 64), :], R2.at[s * 3 + dx - 1],
                      s2.at[s, dx], r2.at[s * 3 + dx - 1], cid(z, yl, to), tp)

    def r2z_copy(s, line, dz, dy, b):
        slot = ((3 - dz) * 2 + dy) * 4 + b
        return remote(L.at[tile_of(k, line), 64 * b:64 * b + 64, :], R2.at[slot],
                      s2.at[s, b], r2.at[slot], cid((z + dz) % 4, yl, x), tp)

    def r2_each(s, line, do):
        dz, dy = order(s)

        @pl.when((k == 0))
        def _():
            for dx in (1, 3, 2):
                do(r2x_copy(s, line, dx))

        @pl.when((k == 1) & (dz > 0))
        def _():
            for b in range(4):
                do(r2z_copy(s, line, dz, dy, b))

    def r3x_copy(s, to):
        dz, dy = order(s)
        slot = ((4 - dz) % 4) * 4 + dy * 2 + (yh + to) % 2
        return remote(R3s.at[s, 32 * to:32 * to + 32, :], R3.at[slot], s3.at[s, to], r3.at[slot],
                      cid((z + dz) % 4, (yl + dy) % 2, x), to * 2 + k)

    def r3x_each(s, do):
        for to in range(2):
            @pl.when((s > 0) | (yh != to))
            def _():
                do(r3x_copy(s, to))

    def finish_x(s):
        dz, dy = order(s)
        line = line_at(dz, dy)
        for dx in (1, 2, 3):
            r2x_copy(s, line, dx).wait_recv()
        total = L[tile_of(k, line), pl.ds(block_at(x), 64), :].astype(F32)
        for dx in range(3):
            total = total + R2[s * 3 + dx].astype(F32)
        R3s[s] = total.astype(BF16)
        r3x_each(s, lambda copy: copy.start())

        @pl.when(s == 0)
        def _():
            R3[0] = R3s[0, pl.ds(pl.multiple_of(32 * yh, 32), 32), :]

    def r3z_copy(dx, dy, to):
        at = L.at[tile_of(k, line_at(0, dy)), pl.ds(pl.multiple_of(block_at((x + dx) % 4) + 32 * to, 32), 32), :]
        slot = ((4 - dx) % 4) * 4 + dy * 2 + (yh + to) % 2
        return remote(at, R3.at[slot], s3.at[dx * 2 + dy, to], r3.at[slot],
                      cid(z, (yl + dy) % 2, (x + dx) % 4), to * 2 + k)

    def z_any(dy):
        return (yl + dy) % 2 + z >= yl

    def r3z_each(dy, do):
        for dx in (2, 1, 3, 0):
            for to in range(2):
                if dx == 0 and dy == 0:
                    @pl.when(yh != to)
                    def _():
                        do(r3z_copy(dx, dy, to))
                else:
                    do(r3z_copy(dx, dy, to))

    def finish_z(dy):
        line = line_at(0, dy)

        @pl.when(z_any(dy))
        def _():
            t = tile_of(k, line)

            @pl.when(line >= t0)
            def _():
                acc[...] = L[t].astype(F32)

            @pl.when(line < t0)
            def _():
                acc[...] = jnp.zeros_like(acc)

            for off in (1, 2, 3):
                @pl.when((z + off) % 4 < z)
                def _():
                    for b in range(4):
                        slot = ((off - 1) * 2 + dy) * 4 + b
                        at = R2.at[slot]
                        remote(at, at, s2.at[0, 0], r2.at[slot], c, sib).wait_recv()
                        acc[64 * b:64 * b + 64, :] += at[...].astype(F32)

            L[t] = acc[...].astype(BF16)
            r3z_each(dy, lambda copy: copy.start())
            if dy == 0:
                R3[0] = L[t, pl.ds(pl.multiple_of(block_at(x) + 32 * yh, 32), 32), :]

    @pl.loop(0, 8)
    def _(i):
        s = 7 - i
        dz, dy = order(s)
        line = line_at(dz, dy)

        @pl.loop(0, 2)
        def _(kk):
            kind = (k + 1 - kk) % 2
            t = tile_of(kind, line)

            @pl.when((kk == 1) & (s < 6) & (k == 0))
            def _():
                finish_x(s + 2)

            @pl.when(active(kind, line))
            def _():
                acc[...] = jnp.zeros_like(acc)

                @pl.loop(0, 2)
                def _(i):
                    @pl.when((i == 0) | (t <= t0))
                    def _():
                        backward(t, 1 - i)

                @pl.when(kk == 0)
                def _():
                    L[t] = acc[...].astype(BF16)
                    r1_copy(s, line).start()

                @pl.when(kk == 1)
                def _():
                    remote(L.at[t], R1.at[s], s1.at[s], r1.at[s], c, sib).wait_recv()
                    L[t] = (acc[...] + R1[s].astype(F32)).astype(BF16)
                    r2_each(s, line, lambda copy: copy.start())

    @pl.when(k == 1)
    def _():
        finish_z(1)
        finish_z(0)

    @pl.loop(0, 8)
    def _(p):
        cols = pl.ds(pl.multiple_of(p * 128, 128), 128)
        ob = [O[hf, :, cols].T.astype(BF16) for hf in range(2)]
        db = [DA[hf, :, cols].T.astype(BF16) for hf in range(2)]
        for e in range(2):
            r = slice(64 * e, 64 * e + 64)
            h = 2 * p + e
            o = jnp.concatenate([ob[0][r], ob[1][r]], axis=0)
            d = jnp.concatenate([db[0][r], db[1][r]], axis=0)
            rows = pl.ds(h, 128, stride=16)
            X[0, rows, :] = dot(o, wv[h])
            X[1, rows, :] = dot_nt(d[:, :512], wk[h])
            qr[h] = d[:, 512:].astype(F32).T.astype(BF16)

        @pl.when((p == 0) & (k == 0))
        def _():
            finish_x(1)
            finish_x(0)

    stores = []
    q[...] = X[0].astype(BF16)
    og[...] = X[1].astype(BF16)
    for i, (ref, out) in enumerate(((q, attn_hbm), (og, gq_hbm), (qr, gqr_hbm))):
        stores.append(pltpu.make_async_copy(ref, out, sout.at[i]))
        stores[i].start()

    my_rows = pl.ds(pl.multiple_of(64 * k + 32 * yh, 32), 32)
    fin[my_rows, :] = R3[0].astype(F32)

    @pl.loop(1, 16)
    def _(slot):
        @pl.when((k == 0) | (z + yl >= (yl + (slot // 2) % 2) % 2))
        def _():
            at = R3.at[slot]
            remote(at, at, s3.at[0, 0], r3.at[slot], c, sib).wait_recv()
            fin[my_rows, :] += at[...].astype(F32)

    def r4_copy(j):
        at = fin.at[my_rows, :]
        return remote(at, at, s4.at[j - 1], r4.at[j - 1], c, ((yh + j // 2) % 2) * 2 + (k + j % 2) % 2)

    for j in (1, 2, 3):
        r4_copy(j).start()

    @pl.loop(0, 8)
    def _(s):
        dz, dy = order(s)
        line = line_at(dz, dy)

        @pl.when(active(1 - k, line))
        def _():
            r1_copy(s, line).wait_send()

        @pl.when(active(k, line))
        def _():
            r2_each(s, line, lambda copy: copy.wait_send())

        @pl.when(k == 0)
        def _():
            r3x_each(s, lambda copy: copy.wait_send())

    @pl.when(k == 1)
    def _():
        for dy in range(2):
            @pl.when(z_any(dy))
            def _():
                r3z_each(dy, lambda copy: copy.wait_send())

    for j in (1, 2, 3):
        r4_copy(j).wait()
    flip[...] = fin[...].T
    stores.append(pltpu.make_async_copy(flip, gl_hbm, sout.at[3]))
    stores[3].start()
    for store in stores:
        store.wait()


DMA = pltpu.SemaphoreType.DMA
SCRATCH = [
    pltpu.VMEM((576, 128), BF16),
    pltpu.VMEM((2048, 128), BF16),
    pltpu.VMEM((16, 64, 128), BF16),
    pltpu.VMEM((2048, 128), BF16),
    pltpu.VMEM((16, 128, 512), BF16),
    pltpu.VMEM((16, 512, 128), BF16),
    pltpu.VMEM((2, 2048, 128), F32),
    DMA((6,)), DMA((4,)),
    pltpu.VMEM((16, 256, 576), BF16),
    pltpu.VMEM((16, 576, 256), BF16),
    pltpu.VMEM((2, 1024, 576), BF16),
    pltpu.VMEM((2, 576, 1024), BF16),
    pltpu.VMEM((2, 1024, 512), BF16),
    pltpu.VMEM((2, 512, 1024), BF16),
    pltpu.VMEM((17, 256, 1024), F32),
    pltpu.VMEM((2, 512, 1024), F32),
    pltpu.VMEM((2, 576, 1024), F32),
    pltpu.VMEM((2, 1, 1024), F32),
    pltpu.VMEM((2, 1, 1024), F32),
    pltpu.VMEM((2, 1, 1024), F32),
    pltpu.VMEM((2, 1, 1024), F32),
    pltpu.VMEM((256, 1024), BF16),
    pltpu.VMEM((256, 1024), BF16),
    pltpu.VMEM((256, 576), F32),
    pltpu.VMEM((8, 256, 576), BF16),
    pltpu.VMEM((24, 64, 576), BF16),
    pltpu.VMEM((8, 64, 576), BF16),
    pltpu.VMEM((16, 32, 576), BF16),
    pltpu.VMEM((128, 576), F32),
    pltpu.VMEM((576, 128), F32),
    DMA((3,)), DMA((3,)), DMA((3,)), DMA((3,)), DMA((3, 3)), DMA((3, 3)), DMA((4, 2)), DMA((4, 2)), DMA((8,)), DMA((8,)),
    DMA((8,)), DMA((8,)), DMA((8, 4)), DMA((24,)), DMA((8, 2)), DMA((16,)), DMA((3,)), DMA((3,)),
]


def body(q_nope, q_rope, latent, up_keys, up_values, out_grad):
    def flat(v):
        return v.reshape(2048, v.shape[2])

    hbm = pl.BlockSpec(memory_space=pl.ANY)
    attn, gq, gqr, gl = pl.pallas_call(
        kernel,
        out_shape=[
            jax.ShapeDtypeStruct((2048, 128), BF16),
            jax.ShapeDtypeStruct((2048, 128), BF16),
            jax.ShapeDtypeStruct((16, 64, 128), BF16),
            jax.ShapeDtypeStruct((576, 128), F32),
        ],
        in_specs=[hbm] * 6,
        out_specs=[hbm] * 4,
        scratch_shapes=SCRATCH,
        compiler_params=pltpu.CompilerParams(
            vmem_limit_bytes=63 * 2**20, collective_id=0, has_side_effects=True),
        cost_estimate=pl.CostEstimate(flops=30_000_000_000, bytes_accessed=12_000_000, transcendentals=9_000_000),
    )(latent.T, flat(q_nope), jnp.transpose(q_rope, (1, 2, 0)), flat(out_grad), up_keys, up_values)
    return attn.reshape(128, 16, 128), gq.reshape(128, 16, 128), jnp.transpose(gqr, (2, 0, 1)), gl.T


def solution(mesh):
    rows = P("ctx", "tp", None)
    return jax.shard_map(
        body, mesh=mesh,
        in_specs=(rows, rows, P("ctx", None), P("tp", None, None), P("tp", None, None), rows),
        out_specs=(rows, rows, rows, P("ctx", None)),
        check_vma=False,
    )
```

```python
import math

import jax
import jax.numpy as jnp
from jax import lax
from jax.experimental import pallas as pl
from jax.experimental.pallas import tpu as pltpu
from jax.sharding import PartitionSpec as P

F32, BF16 = jnp.float32, jnp.bfloat16
SCALE = 192**-0.5
LOG2_SCALE = SCALE * math.log2(math.e)
NEG = -1e30
MESH = pl.DeviceIdType.MESH


def dot(a, b):
    return jnp.dot(a, b, preferred_element_type=F32)


def dot_nt(a, b):
    return lax.dot_general(a, b, (((1,), (1,)), ((), ())), preferred_element_type=F32)


def remote(src, dst, send_sem, recv_sem, ctx, tp):
    return pltpu.make_async_remote_copy(
        src_ref=src, dst_ref=dst, send_sem=send_sem, recv_sem=recv_sem,
        device_id={"ctx": ctx, "tp": tp}, device_id_type=MESH,
    )


def kernel(lat_hbm, q_hbm, qr_hbm, og_hbm, wk_hbm, wv_hbm, attn_hbm, gq_hbm, gqr_hbm, gl_hbm,
           lat, q, qr, og, wk, wv, sin, sout,
           L, LT, A, AT, G, GT, SA, SB, O, DA, top, tot, lse, delta, dsb, pbb, acc,
           R1, R2, R3s, R3, fin, flip,
           sx, rx, sz, rz, sb, rb, sy, ry, ss, rs, s1, r1, s2, r2, s3, r3, s4, r4):
    c, tp = lax.axis_index("ctx"), lax.axis_index("tp")
    z, yl, x = c // 8, (c // 4) % 2, c % 4
    yh, k = tp // 2, tp % 2
    t0 = c // 4
    sib = yh * 2 + 1 - k

    def cid(z_, yl_, x_):
        return z_ * 8 + yl_ * 4 + x_

    def tile_of(kind, line):
        return jnp.where(kind == 0, line, 15 - line)

    def block_at(x_):
        return pl.multiple_of(64 * jnp.where(k == 0, x_, 3 - x_), 64)

    def order(s):
        i = jnp.where(s >= 5, s - 4, s - 1)
        dz = i + jnp.where(i == 2, 1, 0) - jnp.where(i == 3, 1, 0)
        return jnp.where(s <= 1, 0, dz), jnp.where((s == 1) | (s >= 5), 1, 0)

    def line_at(dz, dy):
        return 2 * ((z + dz) % 4) + (yl + dy) % 2

    def active(kind, line):
        return (kind == 0) | (line >= t0)

    mine = tile_of(k, t0)
    loads = [
        pltpu.make_async_copy(src, dst, sin.at[i]) for i, (src, dst) in enumerate((
            (lat_hbm, lat),
            (q_hbm, q), (wk_hbm, wk), (qr_hbm, qr), (og_hbm, og), (wv_hbm, wv)))
    ]
    for load in loads:
        load.start()

    barrier = pltpu.get_barrier_semaphore()

    def hello(ctx, tp_):
        pl.semaphore_signal(barrier, inc=1, device_id={"ctx": ctx, "tp": tp_}, device_id_type=MESH)

    @pl.loop(1, 4)
    def _(i):
        hello(cid(z, yl, (x + i) % 4), tp)

    @pl.loop(1, 16)
    def _(i):
        hello(cid((z + i // 4) % 4, (yl + (i // 2) % 2) % 2, x), ((yh + i % 2) % 2) * 2 + k)

    hello(c, sib)
    hello(c, (1 - yh) * 2 + 1 - k)
    pl.semaphore_wait(barrier, 20)

    def x_copy(dx):
        at = L.at[mine, pl.ds(block_at(x), 64), :]
        return remote(at, at, sx.at[dx - 1], rx.at[dx - 1], cid(z, yl, (x + dx) % 4), tp)

    def z_copy(dz, part):
        at = L.at[mine, pl.ds(pl.multiple_of(128 * ((yh + part) % 2), 128), 128), :]
        return remote(at, at, sz.at[dz - 1, part], rz.at[3 - dz, part], cid((z + dz) % 4, yl, x), tp)

    def zb_copy(dz):
        at = L.at[mine, pl.ds(block_at(x), 64), :]
        return remote(at, at, sz.at[dz - 1, 0], rz.at[3 - dz, 0], cid((z + dz) % 4, yl, x), tp)

    def xb_copy(dz, dx):
        at = L.at[tile_of(k, line_at(dz, 0)), pl.ds(block_at(x), 64), :]
        return remote(at, at, sb.at[dz - 1, dx - 1], rb.at[dz - 1, dx - 1], cid(z, yl, (x + dx) % 4), tp)

    def xb_arrive(dz):
        for dx in (1, 3, 2):
            xb_copy(dz, dx).wait_recv()

    def z_arrive(dz, part):
        z_copy(4 - dz, part).wait_recv()

    def y_copy(dz, to):
        at = L.at[tile_of(k, line_at(dz, 0)), pl.ds(pl.multiple_of(128 * yh, 128), 128), :]
        return remote(at, at, sy.at[dz, to], ry.at[dz, yh], cid(z, 1 - yl, x), to * 2 + k)

    def core_copy(s, line):
        at = L.at[tile_of(k, line)]
        return remote(at, at, ss.at[s], rs.at[s], c, sib)

    loads[0].wait()
    fin[...] = lat[...].astype(F32).T
    L[mine, pl.ds(block_at(x), 64), :] = fin[pl.ds(pl.multiple_of(64 * k, 64), 64), :].astype(BF16)
    for dx in (1, 3, 2):
        x_copy(dx).start()

    @pl.when(k == 1)
    def _():
        for dz in (1, 3, 2):
            zb_copy(dz).start()

    for load in loads[1:]:
        load.wait()
    SA[0:2048] = q[...].astype(F32)
    SA[2048:4096] = og[...].astype(F32)

    def head(i, h):
        return SA[pl.ds(2048 * i + h, 128, stride=16), :]

    @pl.loop(0, 8)
    def _(p):
        cols = pl.ds(pl.multiple_of(p * 128, 128), 128)
        pa = dot(head(0, 2 * p).astype(BF16), wk[2 * p])
        pb = dot(head(0, 2 * p + 1).astype(BF16), wk[2 * p + 1])
        ga = dot_nt(head(1, 2 * p).astype(BF16), wv[2 * p])
        gb = dot_nt(head(1, 2 * p + 1).astype(BF16), wv[2 * p + 1])
        ra, rb = qr[2 * p].astype(F32).T, qr[2 * p + 1].astype(F32).T
        for hf in range(2):
            r = slice(64 * hf, 64 * hf + 64)
            blk = jnp.concatenate([pa[r], pb[r]], axis=0)
            A[hf, cols, :512] = blk.astype(BF16)
            AT[hf, :512, cols] = blk.T.astype(BF16)
            rblk = jnp.concatenate([ra[r], rb[r]], axis=0)
            A[hf, cols, 512:] = rblk.astype(BF16)
            AT[hf, 512:, cols] = rblk.T.astype(BF16)
            gblk = jnp.concatenate([ga[r], gb[r]], axis=0)
            G[hf, cols, :] = gblk.astype(BF16)
            GT[hf, :, cols] = gblk.T.astype(BF16)

    top[...] = jnp.full_like(top, NEG)
    tot[...] = jnp.zeros_like(tot)
    O[...] = jnp.zeros_like(O)
    DA[...] = jnp.zeros_like(DA)

    def units_of(line):
        early = line <= t0
        return ((0, line, 1, SA, line * 2048),
                (1, jnp.where(early, line, 15 - line), jnp.where(early, 0, 1), SB, line * 2048))

    third = (1, 15 - t0, 1, SB, 8 * 2048)

    def score_at(row, ch, j):
        return pl.ds(pl.multiple_of(row + ch * 512 + j * 256, 256), 256)

    def score_load(ref, row, ch):
        return jnp.concatenate([ref[score_at(row, ch, 0), :], ref[score_at(row, ch, 1), :]], axis=1)

    def scores(unit, masked):
        u, t, hf, ref, row = unit
        for ch in range(4):
            cs = slice(ch * 256, ch * 256 + 256)
            v = dot(L[t], AT[hf, :, cs]) * LOG2_SCALE
            if masked:
                base = jnp.where(hf == 1, 63 - c, c) * 64 - t * 256
                diff = lax.broadcasted_iota(jnp.int32, (256, 256), 0) - lax.rem(
                    lax.broadcasted_iota(jnp.int32, (256, 256), 1), 64)
                v = jnp.where(diff <= base, v, NEG)
            ref[score_at(row, ch, 0), :] = v[:, :128]
            ref[score_at(row, ch, 1), :] = v[:, 128:]

    def values(unit):
        u, t, hf, ref, row = unit
        shrink = []
        for ch in range(4):
            cs = slice(ch * 256, ch * 256 + 256)
            v = score_load(ref, row, ch)
            old = top[hf, :, cs]
            new = jnp.maximum(old, jnp.max(v, axis=0, keepdims=True))
            p = jnp.exp2(v - new)
            al = jnp.exp2(old - new)
            top[hf, :, cs] = new
            tot[hf, :, cs] = tot[hf, :, cs] * al + jnp.sum(p, axis=0, keepdims=True)
            pbb[u, :, cs] = p.astype(BF16)
            shrink.append(al)
        for ch in range(4):
            cs = slice(ch * 256, ch * 256 + 256)
            O[hf, :, cs] = O[hf, :, cs] * shrink[ch] + dot(LT[t, :512, :], pbb[u, :, cs])

    def sibling_arrives(s, line):
        at = L.at[tile_of(1 - k, line)]
        remote(at, at, ss.at[s], rs.at[s], c, sib).wait_recv()

    for dx in (1, 2, 3):
        x_copy(dx).wait_recv()
    @pl.when(k == 0)
    def _():
        for dz, part in ((1, 0), (3, 0), (1, 1), (3, 1), (2, 0), (2, 1)):
            z_copy(dz, part).start()

    def y_start(dz):
        for to in range(2):
            y_copy(dz, to).start()

    y_start(0)
    core_copy(0, t0).start()

    @pl.when(k == 1)
    def _():
        for dz in (1, 3, 2):
            zb_copy(4 - dz).wait_recv()
            for dx in (1, 3, 2):
                xb_copy(dz, dx).start()

    sibling_arrives(0, t0)
    LT[t0] = L[t0].T
    LT[15 - t0] = L[15 - t0].T
    one, two = units_of(t0)
    scores(one, False)
    scores(two, True)
    values(one)
    values(two)
    scores(third, True)
    values(third)

    def receive(s):
        dz, dy = order(s)
        line = line_at(dz, dy)

        @pl.when((s == 1) & (k == 0))
        def _():
            for dz_ in (1, 3):
                z_arrive(dz_, 0)
                y_start(dz_)

        @pl.when((s == 1) & (k == 1))
        def _():
            xb_arrive(1)
            y_start(1)

        @pl.when((s == 2) & (k == 0))
        def _():
            z_arrive(1, 1)
            z_arrive(3, 1)

        @pl.when((s == 2) & (k == 1))
        def _():
            xb_arrive(3)
            y_start(3)

        @pl.when(s == 2)
        def _():
            core_copy(2, line_at(1, 0)).start()
            core_copy(3, line_at(3, 0)).start()

        @pl.when((s == 3) & (k == 0))
        def _():
            z_arrive(2, 0)
            y_start(2)

        @pl.when((s == 3) & (k == 1))
        def _():
            xb_arrive(2)
            y_start(2)

        @pl.when((s == 4) & (k == 0))
        def _():
            z_arrive(2, 1)

        @pl.when(s == 4)
        def _():
            core_copy(4, line_at(2, 0)).start()

        @pl.when(dy == 1)
        def _():
            for frm in range(2):
                at = L.at[tile_of(k, line), 128 * frm:128 * frm + 128, :]
                remote(at, at, sy.at[dz, 0], ry.at[dz, frm], cid(z, 1 - yl, x), frm * 2 + k).wait_recv()
            core_copy(s, line).start()

    receive(1)

    @pl.loop(1, 8)
    def _(s):
        @pl.when(s < 7)
        def _():
            receive(s + 1)

        dz, dy = order(s)
        line = line_at(dz, dy)
        sibling_arrives(s, line)
        LT[line] = L[line].T

        @pl.when(line > t0)
        def _():
            LT[15 - line] = L[15 - line].T

        one, two = units_of(line)
        scores(one, False)
        scores(two, False)
        values(one)
        values(two)

    for hf in range(2):
        for ch in range(4):
            cs = slice(ch * 256, ch * 256 + 256)
            lse[hf, :, cs] = top[hf, :, cs] + jnp.log2(tot[hf, :, cs])
            inverse = 1.0 / tot[hf, :, cs]
            tot[hf, :, cs] = inverse
            delta[hf, :, cs] = jnp.sum(GT[hf, :, cs].astype(F32) * O[hf, :, cs], axis=0, keepdims=True) * inverse

    for d in (1, 2, 3):
        x_copy(d).wait_send()

        @pl.when(k == 0)
        def _():
            z_copy(d, 0).wait_send()
            z_copy(d, 1).wait_send()

        @pl.when(k == 1)
        def _():
            zb_copy(d).wait_send()
            for dx in (1, 2, 3):
                xb_copy(d, dx).wait_send()

    @pl.loop(0, 8)
    def _(s):
        dz, dy = order(s)

        @pl.when(dy == 0)
        def _():
            for to in range(2):
                y_copy(dz, to).wait_send()

        core_copy(s, line_at(dz, dy)).wait_send()

    def grads(unit):
        u, t, hf, ref, row = unit
        for ch in range(4):
            cs = slice(ch * 256, ch * 256 + 256)
            dp = dot(L[t, :, :512], GT[hf, :, cs])
            p = jnp.exp2(score_load(ref, row, ch) - lse[hf, :, cs])
            dsb[u, :, cs] = (p * (dp - delta[hf, :, cs]) * SCALE).astype(BF16)
            pbb[u, :, cs] = p.astype(BF16)

    def spread(unit):
        u, t, hf, ref, row = unit
        for ch in range(4):
            cs = slice(ch * 256, ch * 256 + 256)
            DA[hf, :, cs] += dot(LT[t], dsb[u, :, cs])
        a, b = dot(dsb[u], A[hf]), dot(pbb[u], G[hf])
        acc[u, :, :512] = a[:, :512] + b
        acc[u, :, 512:] = a[:, 512:]

    def pair(line):
        one, two = units_of(line)
        grads(one)
        grads(two)
        spread(one)
        spread(two)

        @pl.when(line <= t0)
        def _():
            acc[0] += acc[1]

    def r1_copy(s, line):
        return remote(L.at[tile_of(1 - k, line)], R1.at[s], s1.at[s], r1.at[s], c, sib)

    def r2x_copy(s, line, dx):
        to = (x + dx) % 4
        return remote(L.at[tile_of(k, line), pl.ds(block_at(to), 64), :], R2.at[s * 3 + dx - 1],
                      s2.at[s, dx], r2.at[s * 3 + dx - 1], cid(z, yl, to), tp)

    def r2z_copy(s, line, dz, dy, b):
        slot = ((3 - dz) * 2 + dy) * 4 + b
        return remote(L.at[tile_of(k, line), 64 * b:64 * b + 64, :], R2.at[slot],
                      s2.at[s, b], r2.at[slot], cid((z + dz) % 4, yl, x), tp)

    def r2_each(s, line, do):
        dz, dy = order(s)

        @pl.when((k == 0))
        def _():
            for dx in (1, 3, 2):
                do(r2x_copy(s, line, dx))

        @pl.when((k == 1) & (dz > 0))
        def _():
            for b in range(4):
                do(r2z_copy(s, line, dz, dy, b))

    def r3x_copy(s, to):
        dz, dy = order(s)
        slot = ((4 - dz) % 4) * 4 + dy * 2 + (yh + to) % 2
        return remote(R3s.at[s, 32 * to:32 * to + 32, :], R3.at[slot], s3.at[s, to], r3.at[slot],
                      cid((z + dz) % 4, (yl + dy) % 2, x), to * 2 + k)

    def r3x_each(s, do):
        for to in range(2):
            @pl.when((s > 0) | (yh != to))
            def _():
                do(r3x_copy(s, to))

    def finish_x(s):
        dz, dy = order(s)
        line = line_at(dz, dy)
        for dx in (1, 2, 3):
            r2x_copy(s, line, dx).wait_recv()
        total = L[tile_of(k, line), pl.ds(block_at(x), 64), :].astype(F32)
        for dx in range(3):
            total = total + R2[s * 3 + dx].astype(F32)
        R3s[s] = total.astype(BF16)
        r3x_each(s, lambda copy: copy.start())

        @pl.when(s == 0)
        def _():
            R3[0] = R3s[0, pl.ds(pl.multiple_of(32 * yh, 32), 32), :]

    def r3z_copy(dx, dy, to):
        at = L.at[tile_of(k, line_at(0, dy)), pl.ds(pl.multiple_of(block_at((x + dx) % 4) + 32 * to, 32), 32), :]
        slot = ((4 - dx) % 4) * 4 + dy * 2 + (yh + to) % 2
        return remote(at, R3.at[slot], s3.at[dx * 2 + dy, to], r3.at[slot],
                      cid(z, (yl + dy) % 2, (x + dx) % 4), to * 2 + k)

    def z_any(dy):
        return (yl + dy) % 2 + z >= yl

    def r3z_each(dy, do):
        for dx in (2, 1, 3, 0):
            for to in range(2):
                if dx == 0 and dy == 0:
                    @pl.when(yh != to)
                    def _():
                        do(r3z_copy(dx, dy, to))
                else:
                    do(r3z_copy(dx, dy, to))

    def finish_z(dy):
        line = line_at(0, dy)

        @pl.when(z_any(dy))
        def _():
            t = tile_of(k, line)

            @pl.when(line >= t0)
            def _():
                acc[0] = L[t].astype(F32)

            @pl.when(line < t0)
            def _():
                acc[0] = jnp.zeros((256, 576), F32)

            for off in (1, 2, 3):
                @pl.when((z + off) % 4 < z)
                def _():
                    for b in range(4):
                        slot = ((off - 1) * 2 + dy) * 4 + b
                        at = R2.at[slot]
                        remote(at, at, s2.at[0, 0], r2.at[slot], c, sib).wait_recv()
                        acc[0, 64 * b:64 * b + 64, :] += at[...].astype(F32)

            L[t] = acc[0].astype(BF16)
            r3z_each(dy, lambda copy: copy.start())
            if dy == 0:
                R3[0] = L[t, pl.ds(pl.multiple_of(block_at(x) + 32 * yh, 32), 32), :]

    def send_r1(s, line):
        @pl.when(active(1 - k, line))
        def _():
            r1_copy(s, line).start()

    def merge(s):
        dz, dy = order(s)
        line = line_at(dz, dy)

        @pl.when(active(k, line))
        def _():
            t = tile_of(k, line)
            remote(L.at[t], R1.at[s], s1.at[s], r1.at[s], c, sib).wait_recv()
            L[t] = (L[t].astype(F32) + R1[s].astype(F32)).astype(BF16)
            r2_each(s, line, lambda copy: copy.start())

    @pl.loop(0, 7)
    def _(i):
        s = 7 - i
        dz, dy = order(s)
        line = line_at(dz, dy)
        pair(line)
        L[line] = acc[0].astype(BF16)

        @pl.when(line > t0)
        def _():
            L[15 - line] = acc[1].astype(BF16)

        send_r1(s, line)

        @pl.when(i > 0)
        def _():
            merge(s + 1)

        @pl.when((i > 2) & (k == 0))
        def _():
            finish_x(s + 3)

    pair(t0)
    L[t0] = acc[0].astype(BF16)

    @pl.when(k == 1)
    def _():
        send_r1(0, t0)

    grads(third)
    spread(third)
    L[15 - t0] = acc[1].astype(BF16)

    @pl.when(k == 0)
    def _():
        send_r1(0, t0)

    merge(1)

    def token_rows(i, h):
        return pl.ds(2048 * i + h, 128, stride=16)

    def by_head(ref, cols, scale=None):
        both = [ref[hf, :, cols] for hf in range(2)]
        if scale is not None:
            both = [both[hf] * scale[hf, :, cols] for hf in range(2)]
        both = [v.T.astype(BF16) for v in both]
        return [jnp.concatenate([both[0][r], both[1][r]], axis=0) for r in (slice(0, 64), slice(64, 128))]

    @pl.loop(0, 8)
    def _(p):
        o = by_head(O, pl.ds(pl.multiple_of(p * 128, 128), 128), tot)
        for e in range(2):
            SA[token_rows(0, 2 * p + e), :] = dot(o[e], wv[2 * p + e])

    merge(0)

    @pl.when(k == 0)
    def _():
        finish_x(3)
        finish_x(2)
        finish_x(1)

    @pl.when(k == 1)
    def _():
        finish_z(1)
        finish_z(0)

    @pl.loop(0, 8)
    def _(p):
        d = by_head(DA, pl.ds(pl.multiple_of(p * 128, 128), 128))
        for e in range(2):
            SA[token_rows(1, 2 * p + e), :] = dot_nt(d[e][:, :512], wk[2 * p + e])
            qr[2 * p + e] = d[e][:, 512:].astype(F32).T.astype(BF16)

    @pl.when(k == 0)
    def _():
        finish_x(0)

    stores = []
    q[...] = SA[0:2048].astype(BF16)
    og[...] = SA[2048:4096].astype(BF16)
    for i, (ref, out) in enumerate(((q, attn_hbm), (og, gq_hbm), (qr, gqr_hbm))):
        stores.append(pltpu.make_async_copy(ref, out, sout.at[i]))
        stores[i].start()

    my_rows = pl.ds(pl.multiple_of(64 * k + 32 * yh, 32), 32)
    fin[my_rows, :] = R3[0].astype(F32)

    @pl.loop(1, 16)
    def _(slot):
        @pl.when((k == 0) | (z + yl >= (yl + (slot // 2) % 2) % 2))
        def _():
            at = R3.at[slot]
            remote(at, at, s3.at[0, 0], r3.at[slot], c, sib).wait_recv()
            fin[my_rows, :] += at[...].astype(F32)

    def r4_copy(j):
        at = fin.at[my_rows, :]
        return remote(at, at, s4.at[j - 1], r4.at[j - 1], c, ((yh + j // 2) % 2) * 2 + (k + j % 2) % 2)

    for j in (1, 2, 3):
        r4_copy(j).start()

    @pl.loop(0, 8)
    def _(s):
        dz, dy = order(s)
        line = line_at(dz, dy)

        @pl.when(active(1 - k, line))
        def _():
            r1_copy(s, line).wait_send()

        @pl.when(active(k, line))
        def _():
            r2_each(s, line, lambda copy: copy.wait_send())

        @pl.when(k == 0)
        def _():
            r3x_each(s, lambda copy: copy.wait_send())

    @pl.when(k == 1)
    def _():
        for dy in range(2):
            @pl.when(z_any(dy))
            def _():
                r3z_each(dy, lambda copy: copy.wait_send())

    for j in (1, 2, 3):
        r4_copy(j).wait()
    flip[...] = fin[...].T
    stores.append(pltpu.make_async_copy(flip, gl_hbm, sout.at[3]))
    stores[3].start()
    for store in stores:
        store.wait()


DMA = pltpu.SemaphoreType.DMA
SCRATCH = [
    pltpu.VMEM((576, 128), BF16),
    pltpu.VMEM((2048, 128), BF16),
    pltpu.VMEM((16, 64, 128), BF16),
    pltpu.VMEM((2048, 128), BF16),
    pltpu.VMEM((16, 128, 512), BF16),
    pltpu.VMEM((16, 512, 128), BF16),
    DMA((6,)), DMA((4,)),
    pltpu.VMEM((16, 256, 576), BF16),
    pltpu.VMEM((16, 576, 256), BF16),
    pltpu.VMEM((2, 1024, 576), BF16),
    pltpu.VMEM((2, 576, 1024), BF16),
    pltpu.VMEM((2, 1024, 512), BF16),
    pltpu.VMEM((2, 512, 1024), BF16),
    pltpu.VMEM((8 * 2048, 128), F32),
    pltpu.VMEM((9 * 2048, 128), F32),
    pltpu.VMEM((2, 512, 1024), F32),
    pltpu.VMEM((2, 576, 1024), F32),
    pltpu.VMEM((2, 1, 1024), F32),
    pltpu.VMEM((2, 1, 1024), F32),
    pltpu.VMEM((2, 1, 1024), F32),
    pltpu.VMEM((2, 1, 1024), F32),
    pltpu.VMEM((2, 256, 1024), BF16),
    pltpu.VMEM((2, 256, 1024), BF16),
    pltpu.VMEM((2, 256, 576), F32),
    pltpu.VMEM((8, 256, 576), BF16),
    pltpu.VMEM((24, 64, 576), BF16),
    pltpu.VMEM((8, 64, 576), BF16),
    pltpu.VMEM((16, 32, 576), BF16),
    pltpu.VMEM((128, 576), F32),
    pltpu.VMEM((576, 128), F32),
    DMA((3,)), DMA((3,)), DMA((3, 2)), DMA((3, 2)), DMA((3, 3)), DMA((3, 3)), DMA((4, 2)), DMA((4, 2)), DMA((8,)), DMA((8,)),
    DMA((8,)), DMA((8,)), DMA((8, 4)), DMA((24,)), DMA((8, 2)), DMA((16,)), DMA((3,)), DMA((3,)),
]


def hand_over(*refs):
    results, outs, held, sems = refs[:4], refs[4:8], refs[8:12], refs[12]
    loads = [pltpu.make_async_copy(results[i], held[i], sems.at[0, i]) for i in range(4)]
    stores = [pltpu.make_async_copy(held[i], outs[i], sems.at[1, i]) for i in range(4)]
    for load in loads:
        load.start()
    for load, store in zip(loads, stores):
        load.wait()
        store.start()
    for store in stores:
        store.wait()


def body(q_nope, q_rope, latent, up_keys, up_values, out_grad):
    def flat(v):
        return v.reshape(2048, v.shape[2])

    hbm = pl.BlockSpec(memory_space=pl.ANY)
    shapes = [
        jax.ShapeDtypeStruct((2048, 128), BF16),
        jax.ShapeDtypeStruct((2048, 128), BF16),
        jax.ShapeDtypeStruct((16, 64, 128), BF16),
        jax.ShapeDtypeStruct((576, 128), F32),
    ]
    results = pl.pallas_call(
        kernel,
        out_shape=shapes,
        in_specs=[hbm] * 6,
        out_specs=[hbm] * 4,
        scratch_shapes=SCRATCH,
        compiler_params=pltpu.CompilerParams(
            vmem_limit_bytes=63 * 2**20, collective_id=0, has_side_effects=True),
        cost_estimate=pl.CostEstimate(flops=30_000_000_000, bytes_accessed=12_000_000, transcendentals=9_000_000),
    )(latent.T, flat(q_nope), jnp.transpose(q_rope, (1, 2, 0)), flat(out_grad), up_keys, up_values)
    attn, gq, gqr, gl = pl.pallas_call(
        hand_over, out_shape=shapes, in_specs=[hbm] * 4, out_specs=[hbm] * 4,
        scratch_shapes=[pltpu.VMEM(v.shape, v.dtype) for v in shapes] + [DMA((2, 4))],
    )(*results)
    return attn.reshape(128, 16, 128), gq.reshape(128, 16, 128), jnp.transpose(gqr, (2, 0, 1)), gl.T


def solution(mesh):
    rows = P("ctx", "tp", None)
    return jax.shard_map(
        body, mesh=mesh,
        in_specs=(rows, rows, P("ctx", None), P("tp", None, None), P("tp", None, None), rows),
        out_specs=(rows, rows, rows, P("ctx", None)),
        check_vma=False,
    )
```

```python
import math

import jax
import jax.numpy as jnp
from jax import lax
from jax.experimental import pallas as pl
from jax.experimental.pallas import tpu as pltpu
from jax.sharding import PartitionSpec as P

F32, BF16 = jnp.float32, jnp.bfloat16
SCALE = 192**-0.5
LOG2_SCALE = SCALE * math.log2(math.e)
NEG = -1e30
MESH = pl.DeviceIdType.MESH


def dot(a, b):
    return jnp.dot(a, b, preferred_element_type=F32)


def dot_nt(a, b):
    return lax.dot_general(a, b, (((1,), (1,)), ((), ())), preferred_element_type=F32)


def remote(src, dst, send_sem, recv_sem, ctx, tp):
    return pltpu.make_async_remote_copy(
        src_ref=src, dst_ref=dst, send_sem=send_sem, recv_sem=recv_sem,
        device_id={"ctx": ctx, "tp": tp}, device_id_type=MESH,
    )


def kernel(lat_hbm, q_hbm, qr_hbm, og_hbm, wk_hbm, wv_hbm, attn_hbm, gq_hbm, gqr_hbm, gl_hbm,
           lat, q, qr, og, wk, wv, sin, sout,
           L, LT, A, AT, G, GT, SA, SB, O, DA, top, tot, lse, delta, dsb, pbb, acc,
           R1, R2, R3s, R3, fin, whole, flip,
           sx, rx, sz, rz, sb, rb, sy, ry, ss, rs, s1, r1, s2, r2, s3, r3, s4, r4):
    c, tp = lax.axis_index("ctx"), lax.axis_index("tp")
    z, yl, x = c // 8, (c // 4) % 2, c % 4
    yh, k = tp // 2, tp % 2
    t0 = c // 4
    sib = yh * 2 + 1 - k

    def cid(z_, yl_, x_):
        return z_ * 8 + yl_ * 4 + x_

    def tile_of(kind, line):
        return jnp.where(kind == 0, line, 15 - line)

    def block_at(x_):
        return pl.multiple_of(64 * jnp.where(k == 0, x_, 3 - x_), 64)

    def order(s):
        i = jnp.where(s >= 5, s - 4, s - 1)
        dz = i + jnp.where(i == 2, 1, 0) - jnp.where(i == 3, 1, 0)
        return jnp.where(s <= 1, 0, dz), jnp.where((s == 1) | (s >= 5), 1, 0)

    def line_at(dz, dy):
        return 2 * ((z + dz) % 4) + (yl + dy) % 2

    def active(kind, line):
        return (kind == 0) | (line >= t0)

    mine = tile_of(k, t0)
    loads = [
        pltpu.make_async_copy(src, dst, sin.at[i]) for i, (src, dst) in enumerate((
            (lat_hbm, lat),
            (q_hbm, q), (wk_hbm, wk), (qr_hbm, qr), (og_hbm, og), (wv_hbm, wv)))
    ]
    for load in loads:
        load.start()

    barrier = pltpu.get_barrier_semaphore()

    def hello(ctx, tp_):
        pl.semaphore_signal(barrier, inc=1, device_id={"ctx": ctx, "tp": tp_}, device_id_type=MESH)

    @pl.loop(1, 4)
    def _(i):
        hello(cid(z, yl, (x + i) % 4), tp)

    @pl.loop(1, 16)
    def _(i):
        hello(cid((z + i // 4) % 4, (yl + (i // 2) % 2) % 2, x), ((yh + i % 2) % 2) * 2 + k)

    hello(c, sib)
    hello(c, (1 - yh) * 2 + 1 - k)
    loads[0].wait()
    fin[...] = lat[...].astype(F32).T
    L[mine, pl.ds(block_at(x), 64), :] = fin[pl.ds(pl.multiple_of(64 * k, 64), 64), :].astype(BF16)
    pl.semaphore_wait(barrier, 20)

    def x_copy(dx):
        at = L.at[mine, pl.ds(block_at(x), 64), :]
        return remote(at, at, sx.at[dx - 1], rx.at[dx - 1], cid(z, yl, (x + dx) % 4), tp)

    def z_copy(dz, part):
        at = L.at[mine, pl.ds(pl.multiple_of(128 * ((yh + part) % 2), 128), 128), :]
        return remote(at, at, sz.at[dz - 1, part], rz.at[3 - dz, part], cid((z + dz) % 4, yl, x), tp)

    def zb_copy(dz):
        at = L.at[mine, pl.ds(block_at(x), 64), :]
        return remote(at, at, sz.at[dz - 1, 0], rz.at[3 - dz, 0], cid((z + dz) % 4, yl, x), tp)

    def xb_copy(dz, dx):
        at = L.at[tile_of(k, line_at(dz, 0)), pl.ds(block_at(x), 64), :]
        return remote(at, at, sb.at[dz - 1, dx - 1], rb.at[dz - 1, dx - 1], cid(z, yl, (x + dx) % 4), tp)

    def xb_arrive(dz):
        for dx in (1, 3, 2):
            xb_copy(dz, dx).wait_recv()

    def z_arrive(dz, part):
        z_copy(4 - dz, part).wait_recv()

    def y_copy(dz, to):
        at = L.at[tile_of(k, line_at(dz, 0)), pl.ds(pl.multiple_of(128 * yh, 128), 128), :]
        return remote(at, at, sy.at[dz, to], ry.at[dz, yh], cid(z, 1 - yl, x), to * 2 + k)

    def core_copy(s, line):
        at = L.at[tile_of(k, line)]
        return remote(at, at, ss.at[s], rs.at[s], c, sib)

    for dx in (1, 3, 2):
        x_copy(dx).start()

    @pl.when(k == 1)
    def _():
        for dz in (1, 3, 2):
            zb_copy(dz).start()

    for load in loads[1:]:
        load.wait()
    SA[0:2048] = q[...].astype(F32)
    SA[2048:4096] = og[...].astype(F32)

    def head(i, h):
        return SA[pl.ds(2048 * i + h, 128, stride=16), :]

    @pl.loop(0, 8)
    def _(p):
        cols = pl.ds(pl.multiple_of(p * 128, 128), 128)
        pa = dot(head(0, 2 * p).astype(BF16), wk[2 * p])
        pb = dot(head(0, 2 * p + 1).astype(BF16), wk[2 * p + 1])
        ga = dot_nt(head(1, 2 * p).astype(BF16), wv[2 * p])
        gb = dot_nt(head(1, 2 * p + 1).astype(BF16), wv[2 * p + 1])
        ra, rb = qr[2 * p].astype(F32).T, qr[2 * p + 1].astype(F32).T
        for hf in range(2):
            r = slice(64 * hf, 64 * hf + 64)
            blk = jnp.concatenate([pa[r], pb[r]], axis=0)
            A[hf, cols, :512] = blk.astype(BF16)
            AT[hf, :512, cols] = blk.T.astype(BF16)
            rblk = jnp.concatenate([ra[r], rb[r]], axis=0)
            A[hf, cols, 512:] = rblk.astype(BF16)
            AT[hf, 512:, cols] = rblk.T.astype(BF16)
            gblk = jnp.concatenate([ga[r], gb[r]], axis=0)
            G[hf, cols, :] = gblk.astype(BF16)
            GT[hf, :, cols] = gblk.T.astype(BF16)

    top[...] = jnp.full_like(top, NEG)
    tot[...] = jnp.zeros_like(tot)
    O[...] = jnp.zeros_like(O)
    DA[...] = jnp.zeros_like(DA)

    def units_of(line):
        early = line <= t0
        return ((0, line, 1, SA, line * 2048),
                (1, jnp.where(early, line, 15 - line), jnp.where(early, 0, 1), SB, line * 2048))

    third = (1, 15 - t0, 1, SB, 8 * 2048)

    def score_at(row, ch, j):
        return pl.ds(pl.multiple_of(row + ch * 512 + j * 256, 256), 256)

    def score_load(ref, row, ch):
        return jnp.concatenate([ref[score_at(row, ch, 0), :], ref[score_at(row, ch, 1), :]], axis=1)

    def scores(unit, masked):
        u, t, hf, ref, row = unit
        for ch in range(4):
            cs = slice(ch * 256, ch * 256 + 256)
            v = dot(L[t], AT[hf, :, cs]) * LOG2_SCALE
            if masked:
                base = jnp.where(hf == 1, 63 - c, c) * 64 - t * 256
                diff = lax.broadcasted_iota(jnp.int32, (256, 256), 0) - lax.rem(
                    lax.broadcasted_iota(jnp.int32, (256, 256), 1), 64)
                v = jnp.where(diff <= base, v, NEG)
            ref[score_at(row, ch, 0), :] = v[:, :128]
            ref[score_at(row, ch, 1), :] = v[:, 128:]

    def values(unit):
        u, t, hf, ref, row = unit
        shrink = []
        for ch in range(4):
            cs = slice(ch * 256, ch * 256 + 256)
            v = score_load(ref, row, ch)
            old = top[hf, :, cs]
            new = jnp.maximum(old, jnp.max(v, axis=0, keepdims=True))
            p = jnp.exp2(v - new)
            al = jnp.exp2(old - new)
            top[hf, :, cs] = new
            tot[hf, :, cs] = tot[hf, :, cs] * al + jnp.sum(p, axis=0, keepdims=True)
            pbb[u, :, cs] = p.astype(BF16)
            shrink.append(al)
        for ch in range(4):
            cs = slice(ch * 256, ch * 256 + 256)
            O[hf, :, cs] = O[hf, :, cs] * shrink[ch] + dot(LT[t, :512, :], pbb[u, :, cs])

    def sibling_arrives(s, line):
        at = L.at[tile_of(1 - k, line)]
        remote(at, at, ss.at[s], rs.at[s], c, sib).wait_recv()

    for dx in (1, 2, 3):
        x_copy(dx).wait_recv()
    @pl.when(k == 0)
    def _():
        for dz, part in ((1, 0), (3, 0), (1, 1), (3, 1), (2, 0), (2, 1)):
            z_copy(dz, part).start()

    def y_start(dz):
        for to in range(2):
            y_copy(dz, to).start()

    y_start(0)
    core_copy(0, t0).start()

    @pl.when(k == 1)
    def _():
        for dz in (1, 3, 2):
            zb_copy(4 - dz).wait_recv()
            for dx in (1, 3, 2):
                xb_copy(dz, dx).start()

    sibling_arrives(0, t0)
    LT[t0] = L[t0].T
    LT[15 - t0] = L[15 - t0].T
    one, two = units_of(t0)
    scores(one, False)
    scores(two, True)
    values(one)
    values(two)
    scores(third, True)
    values(third)

    def receive(s):
        dz, dy = order(s)
        line = line_at(dz, dy)

        @pl.when((s == 1) & (k == 0))
        def _():
            for dz_ in (1, 3):
                z_arrive(dz_, 0)
                y_start(dz_)

        @pl.when((s == 1) & (k == 1))
        def _():
            xb_arrive(1)
            y_start(1)

        @pl.when((s == 2) & (k == 0))
        def _():
            z_arrive(1, 1)
            z_arrive(3, 1)

        @pl.when((s == 2) & (k == 1))
        def _():
            xb_arrive(3)
            y_start(3)

        @pl.when(s == 2)
        def _():
            core_copy(2, line_at(1, 0)).start()
            core_copy(3, line_at(3, 0)).start()

        @pl.when((s == 3) & (k == 0))
        def _():
            z_arrive(2, 0)
            y_start(2)

        @pl.when((s == 3) & (k == 1))
        def _():
            xb_arrive(2)
            y_start(2)

        @pl.when((s == 4) & (k == 0))
        def _():
            z_arrive(2, 1)

        @pl.when(s == 4)
        def _():
            core_copy(4, line_at(2, 0)).start()

        @pl.when(dy == 1)
        def _():
            for frm in range(2):
                at = L.at[tile_of(k, line), 128 * frm:128 * frm + 128, :]
                remote(at, at, sy.at[dz, 0], ry.at[dz, frm], cid(z, 1 - yl, x), frm * 2 + k).wait_recv()
            core_copy(s, line).start()

    receive(1)

    @pl.loop(1, 8)
    def _(s):
        @pl.when(s < 7)
        def _():
            receive(s + 1)

        dz, dy = order(s)
        line = line_at(dz, dy)
        sibling_arrives(s, line)
        LT[line] = L[line].T

        @pl.when(line > t0)
        def _():
            LT[15 - line] = L[15 - line].T

        one, two = units_of(line)
        scores(one, False)
        scores(two, False)
        values(one)
        values(two)

    for hf in range(2):
        for ch in range(4):
            cs = slice(ch * 256, ch * 256 + 256)
            lse[hf, :, cs] = top[hf, :, cs] + jnp.log2(tot[hf, :, cs])
            inverse = 1.0 / tot[hf, :, cs]
            tot[hf, :, cs] = inverse
            delta[hf, :, cs] = jnp.sum(GT[hf, :, cs].astype(F32) * O[hf, :, cs], axis=0, keepdims=True) * inverse

    for d in (1, 2, 3):
        x_copy(d).wait_send()

        @pl.when(k == 0)
        def _():
            z_copy(d, 0).wait_send()
            z_copy(d, 1).wait_send()

        @pl.when(k == 1)
        def _():
            zb_copy(d).wait_send()
            for dx in (1, 2, 3):
                xb_copy(d, dx).wait_send()

    @pl.loop(0, 8)
    def _(s):
        dz, dy = order(s)

        @pl.when(dy == 0)
        def _():
            for to in range(2):
                y_copy(dz, to).wait_send()

        core_copy(s, line_at(dz, dy)).wait_send()

    def grads(unit, d):
        u, t, hf, ref, row = unit
        for ch in range(4):
            cs = slice(ch * 256, ch * 256 + 256)
            dp = dot(L[t, :, :512], GT[hf, :, cs])
            p = jnp.exp2(score_load(ref, row, ch) - lse[hf, :, cs])
            dsb[d, :, cs] = (p * (dp - delta[hf, :, cs]) * SCALE).astype(BF16)
            pbb[u, :, cs] = p.astype(BF16)

    def to_queries(unit, d):
        u, t, hf, ref, row = unit
        for ch in range(4):
            cs = slice(ch * 256, ch * 256 + 256)
            DA[hf, :, cs] += dot(LT[t], dsb[d, :, cs])

    def to_keys(unit, d):
        u, t, hf, ref, row = unit
        a, b = dot(dsb[d], A[hf]), dot(pbb[u], G[hf])
        acc[u, :, :512] = a[:, :512] + b
        acc[u, :, 512:] = a[:, 512:]

    def r1_copy(s, line):
        return remote(L.at[tile_of(1 - k, line)], R1.at[s], s1.at[s], r1.at[s], c, sib)

    def r2x_copy(s, line, dx):
        to = (x + dx) % 4
        return remote(L.at[tile_of(k, line), pl.ds(block_at(to), 64), :], R2.at[s * 3 + dx - 1],
                      s2.at[s, dx], r2.at[s * 3 + dx - 1], cid(z, yl, to), tp)

    def r2z_copy(s, line, dz, dy, b):
        slot = ((3 - dz) * 2 + dy) * 4 + b
        return remote(L.at[tile_of(k, line), 64 * b:64 * b + 64, :], R2.at[slot],
                      s2.at[s, b], r2.at[slot], cid((z + dz) % 4, yl, x), tp)

    def r2_each(s, line, do):
        dz, dy = order(s)

        @pl.when((k == 0))
        def _():
            for dx in (1, 3, 2):
                do(r2x_copy(s, line, dx))

        @pl.when((k == 1) & (dz > 0))
        def _():
            for b in range(4):
                do(r2z_copy(s, line, dz, dy, b))

    def r3x_copy(s, to):
        dz, dy = order(s)
        slot = ((4 - dz) % 4) * 4 + dy * 2 + (yh + to) % 2
        return remote(R3s.at[s, 32 * to:32 * to + 32, :], R3.at[slot], s3.at[s, to], r3.at[slot],
                      cid((z + dz) % 4, (yl + dy) % 2, x), to * 2 + k)

    def r3x_each(s, do):
        for to in range(2):
            @pl.when((s > 0) | (yh != to))
            def _():
                do(r3x_copy(s, to))

    def finish_x(s):
        dz, dy = order(s)
        line = line_at(dz, dy)
        for dx in (1, 2, 3):
            r2x_copy(s, line, dx).wait_recv()
        total = L[tile_of(k, line), pl.ds(block_at(x), 64), :].astype(F32)
        for dx in range(3):
            total = total + R2[s * 3 + dx].astype(F32)
        R3s[s] = total.astype(BF16)
        r3x_each(s, lambda copy: copy.start())

        @pl.when(s == 0)
        def _():
            R3[0] = R3s[0, pl.ds(pl.multiple_of(32 * yh, 32), 32), :]

    def r3z_copy(dx, dy, to):
        at = L.at[tile_of(k, line_at(0, dy)), pl.ds(pl.multiple_of(block_at((x + dx) % 4) + 32 * to, 32), 32), :]
        slot = ((4 - dx) % 4) * 4 + dy * 2 + (yh + to) % 2
        return remote(at, R3.at[slot], s3.at[dx * 2 + dy, to], r3.at[slot],
                      cid(z, (yl + dy) % 2, (x + dx) % 4), to * 2 + k)

    def z_any(dy):
        return (yl + dy) % 2 + z >= yl

    def r3z_each(dy, do):
        for dx in (2, 1, 3, 0):
            for to in range(2):
                if dx == 0 and dy == 0:
                    @pl.when(yh != to)
                    def _():
                        do(r3z_copy(dx, dy, to))
                else:
                    do(r3z_copy(dx, dy, to))

    def finish_z(dy):
        line = line_at(0, dy)

        @pl.when(z_any(dy))
        def _():
            t = tile_of(k, line)

            @pl.when(line >= t0)
            def _():
                acc[0] = L[t].astype(F32)

            @pl.when(line < t0)
            def _():
                acc[0] = jnp.zeros((256, 576), F32)

            for off in (1, 2, 3):
                @pl.when((z + off) % 4 < z)
                def _():
                    for b in range(4):
                        slot = ((off - 1) * 2 + dy) * 4 + b
                        at = R2.at[slot]
                        remote(at, at, s2.at[0, 0], r2.at[slot], c, sib).wait_recv()
                        acc[0, 64 * b:64 * b + 64, :] += at[...].astype(F32)

            L[t] = acc[0].astype(BF16)
            r3z_each(dy, lambda copy: copy.start())
            if dy == 0:
                R3[0] = L[t, pl.ds(pl.multiple_of(block_at(x) + 32 * yh, 32), 32), :]

    def send_r1(s, line):
        @pl.when(active(1 - k, line))
        def _():
            r1_copy(s, line).start()

    def merge(s):
        dz, dy = order(s)
        line = line_at(dz, dy)

        @pl.when(active(k, line))
        def _():
            t = tile_of(k, line)
            remote(L.at[t], R1.at[s], s1.at[s], r1.at[s], c, sib).wait_recv()
            L[t] = (L[t].astype(F32) + R1[s].astype(F32)).astype(BF16)
            r2_each(s, line, lambda copy: copy.start())

    @pl.loop(0, 7)
    def _(i):
        s = 7 - i
        dz, dy = order(s)
        line = line_at(dz, dy)
        one, two = units_of(line)
        grads(one, 0)
        grads(two, 1)
        to_queries(one, 0)
        to_keys(one, 0)
        to_queries(two, 1)
        to_keys(two, 1)

        @pl.when(line < t0)
        def _():
            acc[0] += acc[1]

        L[line] = acc[0].astype(BF16)

        @pl.when(line > t0)
        def _():
            L[15 - line] = acc[1].astype(BF16)

        send_r1(s, line)

        @pl.when(i > 0)
        def _():
            merge(s + 1)

        @pl.when((i > 3) & (k == 0))
        def _():
            finish_x(s + 4)

    one, two = units_of(t0)
    grads(one, 0)
    grads(two, 1)
    to_keys(one, 0)
    to_keys(two, 1)
    L[t0] = (acc[0] + acc[1]).astype(BF16)

    @pl.when(k == 1)
    def _():
        send_r1(0, t0)

    merge(1)

    @pl.when(k == 0)
    def _():
        finish_x(4)

    @pl.when(k == 1)
    def _():
        finish_z(1)

    grads(third, 2)
    to_keys(third, 2)
    L[15 - t0] = acc[1].astype(BF16)

    @pl.when(k == 0)
    def _():
        send_r1(0, t0)

    @pl.when(k == 0)
    def _():
        merge(0)
        finish_x(3)

    to_queries(one, 0)
    to_queries(two, 1)
    to_queries(third, 2)

    @pl.when(k == 1)
    def _():
        merge(0)
        finish_z(0)

    @pl.when(k == 0)
    def _():
        finish_x(2)
        finish_x(1)

    def token_rows(i, h):
        return pl.ds(2048 * i + h, 128, stride=16)

    def by_head(ref, cols, scale=None):
        both = [ref[hf, :, cols] for hf in range(2)]
        if scale is not None:
            both = [both[hf] * scale[hf, :, cols] for hf in range(2)]
        both = [v.T.astype(BF16) for v in both]
        return [jnp.concatenate([both[0][r], both[1][r]], axis=0) for r in (slice(0, 64), slice(64, 128))]

    @pl.loop(0, 8)
    def _(p):
        o = by_head(O, pl.ds(pl.multiple_of(p * 128, 128), 128), tot)
        for e in range(2):
            SA[token_rows(0, 2 * p + e), :] = dot(o[e], wv[2 * p + e])

    @pl.when(k == 0)
    def _():
        finish_x(0)

    @pl.loop(0, 8)
    def _(p):
        d = by_head(DA, pl.ds(pl.multiple_of(p * 128, 128), 128))
        for e in range(2):
            SA[token_rows(1, 2 * p + e), :] = dot_nt(d[e][:, :512], wk[2 * p + e])
            qr[2 * p + e] = d[e][:, 512:].astype(F32).T.astype(BF16)

    stores = []
    q[...] = SA[0:2048].astype(BF16)
    og[...] = SA[2048:4096].astype(BF16)
    for i, (ref, out) in enumerate(((q, attn_hbm), (og, gq_hbm), (qr, gqr_hbm))):
        stores.append(pltpu.make_async_copy(ref, out, sout.at[i]))
        stores[i].start()

    my_rows = pl.ds(pl.multiple_of(64 * k + 32 * yh, 32), 32)
    fin[my_rows, :] = R3[0].astype(F32)

    @pl.loop(1, 16)
    def _(slot):
        @pl.when((k == 0) | (z + yl >= (yl + (slot // 2) % 2) % 2))
        def _():
            at = R3.at[slot]
            remote(at, at, s3.at[0, 0], r3.at[slot], c, sib).wait_recv()
            fin[my_rows, :] += at[...].astype(F32)

    def r4_copy(j):
        at = whole.at[my_rows, :]
        return remote(at, at, s4.at[j - 1], r4.at[j - 1], c, ((yh + j // 2) % 2) * 2 + (k + j % 2) % 2)

    whole[my_rows, :] = fin[my_rows, :].astype(BF16)
    for j in (1, 2, 3):
        r4_copy(j).start()

    @pl.loop(0, 8)
    def _(s):
        dz, dy = order(s)
        line = line_at(dz, dy)

        @pl.when(active(1 - k, line))
        def _():
            r1_copy(s, line).wait_send()

        @pl.when(active(k, line))
        def _():
            r2_each(s, line, lambda copy: copy.wait_send())

        @pl.when(k == 0)
        def _():
            r3x_each(s, lambda copy: copy.wait_send())

    @pl.when(k == 1)
    def _():
        for dy in range(2):
            @pl.when(z_any(dy))
            def _():
                r3z_each(dy, lambda copy: copy.wait_send())

    for j in (1, 2, 3):
        r4_copy(j).wait()
    flip[...] = whole[...].astype(F32).T
    stores.append(pltpu.make_async_copy(flip, gl_hbm, sout.at[3]))
    stores[3].start()
    for store in stores:
        store.wait()


DMA = pltpu.SemaphoreType.DMA
SCRATCH = [
    pltpu.VMEM((576, 128), BF16),
    pltpu.VMEM((2048, 128), BF16),
    pltpu.VMEM((16, 64, 128), BF16),
    pltpu.VMEM((2048, 128), BF16),
    pltpu.VMEM((16, 128, 512), BF16),
    pltpu.VMEM((16, 512, 128), BF16),
    DMA((6,)), DMA((4,)),
    pltpu.VMEM((16, 256, 576), BF16),
    pltpu.VMEM((16, 576, 256), BF16),
    pltpu.VMEM((2, 1024, 576), BF16),
    pltpu.VMEM((2, 576, 1024), BF16),
    pltpu.VMEM((2, 1024, 512), BF16),
    pltpu.VMEM((2, 512, 1024), BF16),
    pltpu.VMEM((8 * 2048, 128), F32),
    pltpu.VMEM((9 * 2048, 128), F32),
    pltpu.VMEM((2, 512, 1024), F32),
    pltpu.VMEM((2, 576, 1024), F32),
    pltpu.VMEM((2, 1, 1024), F32),
    pltpu.VMEM((2, 1, 1024), F32),
    pltpu.VMEM((2, 1, 1024), F32),
    pltpu.VMEM((2, 1, 1024), F32),
    pltpu.VMEM((3, 256, 1024), BF16),
    pltpu.VMEM((2, 256, 1024), BF16),
    pltpu.VMEM((2, 256, 576), F32),
    pltpu.VMEM((8, 256, 576), BF16),
    pltpu.VMEM((24, 64, 576), BF16),
    pltpu.VMEM((8, 64, 576), BF16),
    pltpu.VMEM((16, 32, 576), BF16),
    pltpu.VMEM((128, 576), F32),
    pltpu.VMEM((128, 576), BF16),
    pltpu.VMEM((576, 128), F32),
    DMA((3,)), DMA((3,)), DMA((3, 2)), DMA((3, 2)), DMA((3, 3)), DMA((3, 3)), DMA((4, 2)), DMA((4, 2)), DMA((8,)), DMA((8,)),
    DMA((8,)), DMA((8,)), DMA((8, 4)), DMA((24,)), DMA((8, 2)), DMA((16,)), DMA((3,)), DMA((3,)),
]


def hand_over(*refs):
    results, outs, held, sems = refs[:4], refs[4:8], refs[8:12], refs[12]
    loads = [pltpu.make_async_copy(results[i], held[i], sems.at[0, i]) for i in range(4)]
    stores = [pltpu.make_async_copy(held[i], outs[i], sems.at[1, i]) for i in range(4)]
    for load in loads:
        load.start()
    for load, store in zip(loads, stores):
        load.wait()
        store.start()
    for store in stores:
        store.wait()


def body(q_nope, q_rope, latent, up_keys, up_values, out_grad):
    def flat(v):
        return v.reshape(2048, v.shape[2])

    hbm = pl.BlockSpec(memory_space=pl.ANY)
    shapes = [
        jax.ShapeDtypeStruct((2048, 128), BF16),
        jax.ShapeDtypeStruct((2048, 128), BF16),
        jax.ShapeDtypeStruct((16, 64, 128), BF16),
        jax.ShapeDtypeStruct((576, 128), F32),
    ]
    results = pl.pallas_call(
        kernel,
        out_shape=shapes,
        in_specs=[hbm] * 6,
        out_specs=[hbm] * 4,
        scratch_shapes=SCRATCH,
        compiler_params=pltpu.CompilerParams(
            vmem_limit_bytes=63 * 2**20, collective_id=0, has_side_effects=True),
        cost_estimate=pl.CostEstimate(flops=30_000_000_000, bytes_accessed=12_000_000, transcendentals=9_000_000),
    )(latent.T, flat(q_nope), jnp.transpose(q_rope, (1, 2, 0)), flat(out_grad), up_keys, up_values)
    attn, gq, gqr, gl = pl.pallas_call(
        hand_over, out_shape=shapes, in_specs=[hbm] * 4, out_specs=[hbm] * 4,
        scratch_shapes=[pltpu.VMEM(v.shape, v.dtype) for v in shapes] + [DMA((2, 4))],
    )(*results)
    return attn.reshape(128, 16, 128), gq.reshape(128, 16, 128), jnp.transpose(gqr, (2, 0, 1)), gl.T


def solution(mesh):
    rows = P("ctx", "tp", None)
    return jax.shard_map(
        body, mesh=mesh,
        in_specs=(rows, rows, P("ctx", None), P("tp", None, None), P("tp", None, None), rows),
        out_specs=(rows, rows, rows, P("ctx", None)),
        check_vma=False,
    )
```

```python
import math

import jax
import jax.numpy as jnp
from jax import lax
from jax.experimental import pallas as pl
from jax.experimental.pallas import tpu as pltpu
from jax.sharding import PartitionSpec as P

F32, BF16 = jnp.float32, jnp.bfloat16
SCALE = 192**-0.5
LOG2_SCALE = SCALE * math.log2(math.e)
NEG = -1e30
MESH = pl.DeviceIdType.MESH


def dot(a, b):
    return jnp.dot(a, b, preferred_element_type=F32)


def dot_nt(a, b):
    return lax.dot_general(a, b, (((1,), (1,)), ((), ())), preferred_element_type=F32)


def remote(src, dst, send_sem, recv_sem, ctx, tp):
    return pltpu.make_async_remote_copy(
        src_ref=src, dst_ref=dst, send_sem=send_sem, recv_sem=recv_sem,
        device_id={"ctx": ctx, "tp": tp}, device_id_type=MESH,
    )


def kernel(lat_hbm, q_hbm, qr_hbm, og_hbm, wk_hbm, wv_hbm, attn_hbm, gq_hbm, gqr_hbm, gl_hbm,
           lat, q, qr, og, wk, wv, sin, sout,
           L, LT, AG, AR, AT, GT, SA, SB, O, DA, top, tot, lse, delta, dp2, acc,
           R1, R2, R3s, R3, fin, whole, flip,
           sx, rx, sz, rz, sb, rb, sy, ry, ss, rs, s1, r1, s2, r2, s3, r3, s4, r4):
    c, tp = lax.axis_index("ctx"), lax.axis_index("tp")
    z, yl, x = c // 8, (c // 4) % 2, c % 4
    yh, k = tp // 2, tp % 2
    t0 = c // 4
    sib = yh * 2 + 1 - k

    def cid(z_, yl_, x_):
        return z_ * 8 + yl_ * 4 + x_

    def tile_of(kind, line):
        return jnp.where(kind == 0, line, 15 - line)

    def block_at(x_):
        return pl.multiple_of(64 * jnp.where(k == 0, x_, 3 - x_), 64)

    def order(s):
        i = jnp.where(s >= 5, s - 4, s - 1)
        dz = i + jnp.where(i == 2, 1, 0) - jnp.where(i == 3, 1, 0)
        return jnp.where(s <= 1, 0, dz), jnp.where((s == 1) | (s >= 5), 1, 0)

    def line_at(dz, dy):
        return 2 * ((z + dz) % 4) + (yl + dy) % 2

    def active(kind, line):
        return (kind == 0) | (line >= t0)

    mine = tile_of(k, t0)
    loads = [
        pltpu.make_async_copy(src, dst, sin.at[i]) for i, (src, dst) in enumerate((
            (lat_hbm, lat),
            (q_hbm, q), (wk_hbm, wk), (qr_hbm, qr), (og_hbm, og), (wv_hbm, wv)))
    ]
    for load in loads:
        load.start()

    barrier = pltpu.get_barrier_semaphore()

    def hello(ctx, tp_):
        pl.semaphore_signal(barrier, inc=1, device_id={"ctx": ctx, "tp": tp_}, device_id_type=MESH)

    @pl.loop(1, 4)
    def _(i):
        hello(cid(z, yl, (x + i) % 4), tp)

    @pl.loop(1, 4)
    def _(i):
        hello(cid((z + i) % 4, yl, x), tp)

    for to in range(2):
        hello(cid(z, 1 - yl, x), to * 2 + k)
    hello(c, sib)
    loads[0].wait()
    fin[...] = lat[...].astype(F32).T
    L[mine, pl.ds(block_at(x), 64), :] = fin[pl.ds(pl.multiple_of(64 * k, 64), 64), :].astype(BF16)
    pl.semaphore_wait(barrier, 9)

    def x_copy(dx):
        at = L.at[mine, pl.ds(block_at(x), 64), :]
        return remote(at, at, sx.at[dx - 1], rx.at[dx - 1], cid(z, yl, (x + dx) % 4), tp)

    def z_copy(dz, part):
        at = L.at[mine, pl.ds(pl.multiple_of(128 * ((yh + part) % 2), 128), 128), :]
        return remote(at, at, sz.at[dz - 1, part], rz.at[3 - dz, part], cid((z + dz) % 4, yl, x), tp)

    def zb_copy(dz):
        at = L.at[mine, pl.ds(block_at(x), 64), :]
        return remote(at, at, sz.at[dz - 1, 0], rz.at[3 - dz, 0], cid((z + dz) % 4, yl, x), tp)

    def xb_copy(dz, dx):
        at = L.at[tile_of(k, line_at(dz, 0)), pl.ds(block_at(x), 64), :]
        return remote(at, at, sb.at[dz - 1, dx - 1], rb.at[dz - 1, dx - 1], cid(z, yl, (x + dx) % 4), tp)

    def xb_arrive(dz):
        for dx in (1, 3, 2):
            xb_copy(dz, dx).wait_recv()

    def z_arrive(dz, part):
        z_copy(4 - dz, part).wait_recv()

    def y_copy(dz, to):
        at = L.at[tile_of(k, line_at(dz, 0)), pl.ds(pl.multiple_of(128 * yh, 128), 128), :]
        return remote(at, at, sy.at[dz, to], ry.at[dz, yh], cid(z, 1 - yl, x), to * 2 + k)

    def core_copy(s, line):
        at = L.at[tile_of(k, line)]
        return remote(at, at, ss.at[s], rs.at[s], c, sib)

    for dx in (1, 3, 2):
        x_copy(dx).start()

    @pl.when(k == 1)
    def _():
        for dz in (1, 3, 2):
            zb_copy(dz).start()

    for load in loads[1:]:
        load.wait()
    SA[0:2048] = q[...].astype(F32)
    SA[2048:4096] = og[...].astype(F32)

    def head(i, h):
        return SA[pl.ds(2048 * i + h, 128, stride=16), :]

    @pl.loop(0, 8)
    def _(p):
        cols = pl.ds(pl.multiple_of(p * 128, 128), 128)
        pa = dot(head(0, 2 * p).astype(BF16), wk[2 * p])
        pb = dot(head(0, 2 * p + 1).astype(BF16), wk[2 * p + 1])
        ga = dot_nt(head(1, 2 * p).astype(BF16), wv[2 * p])
        gb = dot_nt(head(1, 2 * p + 1).astype(BF16), wv[2 * p + 1])
        ra, rb = qr[2 * p].astype(F32).T, qr[2 * p + 1].astype(F32).T
        for hf in range(2):
            r = slice(64 * hf, 64 * hf + 64)
            blk = jnp.concatenate([pa[r], pb[r]], axis=0)
            AG[hf, cols, :] = blk.astype(BF16)
            AT[hf, :512, cols] = blk.T.astype(BF16)
            rblk = jnp.concatenate([ra[r], rb[r]], axis=0)
            AR[hf, cols, :] = rblk.astype(BF16)
            AT[hf, 512:, cols] = rblk.T.astype(BF16)
            gblk = jnp.concatenate([ga[r], gb[r]], axis=0)
            AG[hf, pl.ds(pl.multiple_of(1024 + p * 128, 128), 128), :] = gblk.astype(BF16)
            GT[hf, :, cols] = gblk.T.astype(BF16)

    top[...] = jnp.full_like(top, NEG)
    tot[...] = jnp.zeros_like(tot)
    O[...] = jnp.zeros_like(O)
    DA[...] = jnp.zeros_like(DA)

    def units_of(line):
        early = line <= t0
        return ((0, line, 1, SA, line * 2048),
                (1, jnp.where(early, line, 15 - line), jnp.where(early, 0, 1), SB, line * 2048))

    third = (1, 15 - t0, 1, SB, 8 * 2048)

    def score_at(row, ch, j):
        return pl.ds(pl.multiple_of(row + ch * 512 + j * 256, 256), 256)

    def score_load(ref, row, ch):
        return jnp.concatenate([ref[score_at(row, ch, 0), :], ref[score_at(row, ch, 1), :]], axis=1)

    def scores(unit, masked):
        u, t, hf, ref, row = unit
        for ch in range(4):
            cs = slice(ch * 256, ch * 256 + 256)
            v = dot(L[t], AT[hf, :, cs]) * LOG2_SCALE
            if masked:
                base = jnp.where(hf == 1, 63 - c, c) * 64 - t * 256
                diff = lax.broadcasted_iota(jnp.int32, (256, 256), 0) - lax.rem(
                    lax.broadcasted_iota(jnp.int32, (256, 256), 1), 64)
                v = jnp.where(diff <= base, v, NEG)
            ref[score_at(row, ch, 0), :] = v[:, :128]
            ref[score_at(row, ch, 1), :] = v[:, 128:]

    def values(unit):
        u, t, hf, ref, row = unit
        shrink = []
        for ch in range(4):
            cs = slice(ch * 256, ch * 256 + 256)
            v = score_load(ref, row, ch)
            old = top[hf, :, cs]
            new = jnp.maximum(old, jnp.max(v, axis=0, keepdims=True))
            p = jnp.exp2(v - new)
            al = jnp.exp2(old - new)
            top[hf, :, cs] = new
            tot[hf, :, cs] = tot[hf, :, cs] * al + jnp.sum(p, axis=0, keepdims=True)
            dp2[u, :, 1024 + ch * 256:1280 + ch * 256] = p.astype(BF16)
            shrink.append(al)
        for ch in range(4):
            cs = slice(ch * 256, ch * 256 + 256)
            O[hf, :, cs] = O[hf, :, cs] * shrink[ch] + dot(LT[t, :512, :], dp2[u, :, 1024 + ch * 256:1280 + ch * 256])

    def sibling_arrives(s, line):
        at = L.at[tile_of(1 - k, line)]
        remote(at, at, ss.at[s], rs.at[s], c, sib).wait_recv()

    for dx in (1, 2, 3):
        x_copy(dx).wait_recv()
    @pl.when(k == 0)
    def _():
        for dz, part in ((1, 0), (3, 0), (1, 1), (3, 1), (2, 0), (2, 1)):
            z_copy(dz, part).start()

    def y_start(dz):
        for to in range(2):
            y_copy(dz, to).start()

    y_start(0)
    core_copy(0, t0).start()

    @pl.when(k == 1)
    def _():
        for dz in (1, 3, 2):
            zb_copy(4 - dz).wait_recv()
            for dx in (1, 3, 2):
                xb_copy(dz, dx).start()

    sibling_arrives(0, t0)
    LT[t0] = L[t0].T
    LT[15 - t0] = L[15 - t0].T
    one, two = units_of(t0)
    scores(one, False)
    scores(two, True)
    values(one)
    values(two)
    scores(third, True)
    values(third)

    def receive(s):
        dz, dy = order(s)
        line = line_at(dz, dy)

        @pl.when((s == 1) & (k == 0))
        def _():
            for dz_ in (1, 3):
                z_arrive(dz_, 0)
                y_start(dz_)

        @pl.when((s == 1) & (k == 1))
        def _():
            xb_arrive(1)
            y_start(1)

        @pl.when((s == 2) & (k == 0))
        def _():
            z_arrive(1, 1)
            z_arrive(3, 1)

        @pl.when((s == 2) & (k == 1))
        def _():
            xb_arrive(3)
            y_start(3)

        @pl.when(s == 2)
        def _():
            core_copy(2, line_at(1, 0)).start()
            core_copy(3, line_at(3, 0)).start()

        @pl.when((s == 3) & (k == 0))
        def _():
            z_arrive(2, 0)
            y_start(2)

        @pl.when((s == 3) & (k == 1))
        def _():
            xb_arrive(2)
            y_start(2)

        @pl.when((s == 4) & (k == 0))
        def _():
            z_arrive(2, 1)

        @pl.when(s == 4)
        def _():
            core_copy(4, line_at(2, 0)).start()

        @pl.when(dy == 1)
        def _():
            for frm in range(2):
                at = L.at[tile_of(k, line), 128 * frm:128 * frm + 128, :]
                remote(at, at, sy.at[dz, 0], ry.at[dz, frm], cid(z, 1 - yl, x), frm * 2 + k).wait_recv()
            core_copy(s, line).start()

    receive(1)

    @pl.loop(1, 8)
    def _(s):
        @pl.when(s < 7)
        def _():
            receive(s + 1)

        dz, dy = order(s)
        line = line_at(dz, dy)
        sibling_arrives(s, line)
        LT[line] = L[line].T

        @pl.when(line > t0)
        def _():
            LT[15 - line] = L[15 - line].T

        one, two = units_of(line)
        scores(one, False)
        scores(two, False)
        values(one)
        values(two)

    for hf in range(2):
        for ch in range(4):
            cs = slice(ch * 256, ch * 256 + 256)
            lse[hf, :, cs] = top[hf, :, cs] + jnp.log2(tot[hf, :, cs])
            inverse = 1.0 / tot[hf, :, cs]
            tot[hf, :, cs] = inverse
            delta[hf, :, cs] = jnp.sum(GT[hf, :, cs].astype(F32) * O[hf, :, cs], axis=0, keepdims=True) * inverse

    for d in (1, 2, 3):
        x_copy(d).wait_send()

        @pl.when(k == 0)
        def _():
            z_copy(d, 0).wait_send()
            z_copy(d, 1).wait_send()

        @pl.when(k == 1)
        def _():
            zb_copy(d).wait_send()
            for dx in (1, 2, 3):
                xb_copy(d, dx).wait_send()

    @pl.loop(0, 8)
    def _(s):
        dz, dy = order(s)

        @pl.when(dy == 0)
        def _():
            for to in range(2):
                y_copy(dz, to).wait_send()

        core_copy(s, line_at(dz, dy)).wait_send()

    def grads(unit, d):
        u, t, hf, ref, row = unit
        for ch in range(4):
            cs = slice(ch * 256, ch * 256 + 256)
            dp = dot(L[t, :, :512], GT[hf, :, cs])
            p = jnp.exp2(score_load(ref, row, ch) - lse[hf, :, cs])
            dp2[d, :, cs] = (p * (dp - delta[hf, :, cs]) * SCALE).astype(BF16)
            dp2[d, :, 1024 + ch * 256:1280 + ch * 256] = p.astype(BF16)

    def to_queries(unit, d):
        u, t, hf, ref, row = unit
        for ch in range(4):
            cs = slice(ch * 256, ch * 256 + 256)
            DA[hf, :, cs] += dot(LT[t], dp2[d, :, cs])

    def to_keys(unit, d):
        u, t, hf, ref, row = unit
        acc[u, :, :512] = dot(dp2[d], AG[hf])
        acc[u, :, 512:] = dot(dp2[d, :, :1024], AR[hf])

    def r1_copy(s, line):
        return remote(L.at[tile_of(1 - k, line)], R1.at[s], s1.at[s], r1.at[s], c, sib)

    def r2x_copy(s, line, dx):
        to = (x + dx) % 4
        return remote(L.at[tile_of(k, line), pl.ds(block_at(to), 64), :], R2.at[s * 3 + dx - 1],
                      s2.at[s, dx], r2.at[s * 3 + dx - 1], cid(z, yl, to), tp)

    def r2z_copy(s, line, dz, dy, b):
        slot = ((3 - dz) * 2 + dy) * 4 + b
        return remote(L.at[tile_of(k, line), 64 * b:64 * b + 64, :], R2.at[slot],
                      s2.at[s, b], r2.at[slot], cid((z + dz) % 4, yl, x), tp)

    def r2_each(s, line, do):
        dz, dy = order(s)

        @pl.when((k == 0))
        def _():
            for dx in (1, 3, 2):
                do(r2x_copy(s, line, dx))

        @pl.when((k == 1) & (dz > 0))
        def _():
            for b in range(4):
                do(r2z_copy(s, line, dz, dy, b))

    def r3x_copy(s, to):
        dz, dy = order(s)
        slot = ((4 - dz) % 4) * 4 + dy * 2 + (yh + to) % 2
        return remote(R3s.at[s, 32 * to:32 * to + 32, :], R3.at[slot], s3.at[s, to], r3.at[slot],
                      cid((z + dz) % 4, (yl + dy) % 2, x), to * 2 + k)

    def r3x_each(s, do):
        for to in range(2):
            @pl.when((s > 0) | (yh != to))
            def _():
                do(r3x_copy(s, to))

    def finish_x(s):
        dz, dy = order(s)
        line = line_at(dz, dy)
        for dx in (1, 2, 3):
            r2x_copy(s, line, dx).wait_recv()
        total = L[tile_of(k, line), pl.ds(block_at(x), 64), :].astype(F32)
        for dx in range(3):
            total = total + R2[s * 3 + dx].astype(F32)
        R3s[s] = total.astype(BF16)
        r3x_each(s, lambda copy: copy.start())

        @pl.when(s == 0)
        def _():
            R3[0] = R3s[0, pl.ds(pl.multiple_of(32 * yh, 32), 32), :]

    def r3z_copy(dx, dy, to):
        at = L.at[tile_of(k, line_at(0, dy)), pl.ds(pl.multiple_of(block_at((x + dx) % 4) + 32 * to, 32), 32), :]
        slot = ((4 - dx) % 4) * 4 + dy * 2 + (yh + to) % 2
        return remote(at, R3.at[slot], s3.at[dx * 2 + dy, to], r3.at[slot],
                      cid(z, (yl + dy) % 2, (x + dx) % 4), to * 2 + k)

    def z_any(dy):
        return (yl + dy) % 2 + z >= yl

    def r3z_each(dy, do):
        for dx in (2, 1, 3, 0):
            for to in range(2):
                if dx == 0 and dy == 0:
                    @pl.when(yh != to)
                    def _():
                        do(r3z_copy(dx, dy, to))
                else:
                    do(r3z_copy(dx, dy, to))

    def finish_z(dy):
        line = line_at(0, dy)

        @pl.when(z_any(dy))
        def _():
            t = tile_of(k, line)

            @pl.when(line >= t0)
            def _():
                acc[0] = L[t].astype(F32)

            @pl.when(line < t0)
            def _():
                acc[0] = jnp.zeros((256, 576), F32)

            for off in (1, 2, 3):
                @pl.when((z + off) % 4 < z)
                def _():
                    for b in range(4):
                        slot = ((off - 1) * 2 + dy) * 4 + b
                        at = R2.at[slot]
                        remote(at, at, s2.at[0, 0], r2.at[slot], c, sib).wait_recv()
                        acc[0, 64 * b:64 * b + 64, :] += at[...].astype(F32)

            L[t] = acc[0].astype(BF16)
            r3z_each(dy, lambda copy: copy.start())
            if dy == 0:
                R3[0] = L[t, pl.ds(pl.multiple_of(block_at(x) + 32 * yh, 32), 32), :]

    def send_r1(s, line):
        @pl.when(active(1 - k, line))
        def _():
            r1_copy(s, line).start()

    def merge(s):
        dz, dy = order(s)
        line = line_at(dz, dy)

        @pl.when(active(k, line))
        def _():
            t = tile_of(k, line)
            remote(L.at[t], R1.at[s], s1.at[s], r1.at[s], c, sib).wait_recv()
            L[t] = (L[t].astype(F32) + R1[s].astype(F32)).astype(BF16)
            r2_each(s, line, lambda copy: copy.start())

    @pl.loop(0, 7)
    def _(i):
        s = 7 - i
        dz, dy = order(s)
        line = line_at(dz, dy)
        one, two = units_of(line)
        grads(one, 0)
        grads(two, 1)
        to_queries(one, 0)
        to_keys(one, 0)
        to_queries(two, 1)
        to_keys(two, 1)

        @pl.when(line < t0)
        def _():
            acc[0] += acc[1]

        L[line] = acc[0].astype(BF16)

        @pl.when(line > t0)
        def _():
            L[15 - line] = acc[1].astype(BF16)

        send_r1(s, line)

        @pl.when(i > 0)
        def _():
            merge(s + 1)

        @pl.when((i > 3) & (k == 0))
        def _():
            finish_x(s + 4)

    one, two = units_of(t0)
    grads(one, 0)
    grads(two, 1)
    to_keys(one, 0)
    to_keys(two, 1)
    L[t0] = (acc[0] + acc[1]).astype(BF16)

    @pl.when(k == 1)
    def _():
        send_r1(0, t0)

    merge(1)

    @pl.when(k == 0)
    def _():
        finish_x(4)

    @pl.when(k == 1)
    def _():
        finish_z(1)

    grads(third, 2)
    to_keys(third, 2)
    L[15 - t0] = acc[1].astype(BF16)

    @pl.when(k == 0)
    def _():
        send_r1(0, t0)

    @pl.when(k == 0)
    def _():
        merge(0)
        finish_x(3)

    to_queries(one, 0)
    to_queries(two, 1)
    to_queries(third, 2)

    @pl.when(k == 1)
    def _():
        merge(0)
        finish_z(0)

    @pl.when(k == 0)
    def _():
        finish_x(2)
        finish_x(1)

    def token_rows(i, h):
        return pl.ds(2048 * i + h, 128, stride=16)

    def by_head(ref, cols, scale=None):
        both = [ref[hf, :, cols] for hf in range(2)]
        if scale is not None:
            both = [both[hf] * scale[hf, :, cols] for hf in range(2)]
        both = [v.T.astype(BF16) for v in both]
        return [jnp.concatenate([both[0][r], both[1][r]], axis=0) for r in (slice(0, 64), slice(64, 128))]

    @pl.loop(0, 8)
    def _(p):
        o = by_head(O, pl.ds(pl.multiple_of(p * 128, 128), 128), tot)
        for e in range(2):
            SA[token_rows(0, 2 * p + e), :] = dot(o[e], wv[2 * p + e])

    @pl.when(k == 0)
    def _():
        finish_x(0)

    @pl.loop(0, 8)
    def _(p):
        d = by_head(DA, pl.ds(pl.multiple_of(p * 128, 128), 128))
        for e in range(2):
            SA[token_rows(1, 2 * p + e), :] = dot_nt(d[e][:, :512], wk[2 * p + e])
            qr[2 * p + e] = d[e][:, 512:].astype(F32).T.astype(BF16)

    stores = []
    q[...] = SA[0:2048].astype(BF16)
    og[...] = SA[2048:4096].astype(BF16)
    for i, (ref, out) in enumerate(((q, attn_hbm), (og, gq_hbm), (qr, gqr_hbm))):
        stores.append(pltpu.make_async_copy(ref, out, sout.at[i]))
        stores[i].start()

    my_rows = pl.ds(pl.multiple_of(64 * k + 32 * yh, 32), 32)
    fin[my_rows, :] = R3[0].astype(F32)

    @pl.loop(1, 16)
    def _(slot):
        @pl.when((k == 0) | (z + yl >= (yl + (slot // 2) % 2) % 2))
        def _():
            at = R3.at[slot]
            remote(at, at, s3.at[0, 0], r3.at[slot], c, sib).wait_recv()
            fin[my_rows, :] += at[...].astype(F32)

    def r4_copy(j):
        at = whole.at[my_rows, :]
        return remote(at, at, s4.at[j - 1], r4.at[j - 1], c, ((yh + j // 2) % 2) * 2 + (k + j % 2) % 2)

    whole[my_rows, :] = fin[my_rows, :].astype(BF16)
    for j in (1, 2, 3):
        r4_copy(j).start()

    @pl.loop(0, 8)
    def _(s):
        dz, dy = order(s)
        line = line_at(dz, dy)

        @pl.when(active(1 - k, line))
        def _():
            r1_copy(s, line).wait_send()

        @pl.when(active(k, line))
        def _():
            r2_each(s, line, lambda copy: copy.wait_send())

        @pl.when(k == 0)
        def _():
            r3x_each(s, lambda copy: copy.wait_send())

    @pl.when(k == 1)
    def _():
        for dy in range(2):
            @pl.when(z_any(dy))
            def _():
                r3z_each(dy, lambda copy: copy.wait_send())

    for j in (1, 2, 3):
        r4_copy(j).wait()
    flip[...] = whole[...].astype(F32).T
    stores.append(pltpu.make_async_copy(flip, gl_hbm, sout.at[3]))
    stores[3].start()
    for store in stores:
        store.wait()


DMA = pltpu.SemaphoreType.DMA
SCRATCH = [
    pltpu.VMEM((576, 128), BF16),
    pltpu.VMEM((2048, 128), BF16),
    pltpu.VMEM((16, 64, 128), BF16),
    pltpu.VMEM((2048, 128), BF16),
    pltpu.VMEM((16, 128, 512), BF16),
    pltpu.VMEM((16, 512, 128), BF16),
    DMA((6,)), DMA((4,)),
    pltpu.VMEM((16, 256, 576), BF16),
    pltpu.VMEM((16, 576, 256), BF16),
    pltpu.VMEM((2, 2048, 512), BF16),
    pltpu.VMEM((2, 1024, 64), BF16),
    pltpu.VMEM((2, 576, 1024), BF16),
    pltpu.VMEM((2, 512, 1024), BF16),
    pltpu.VMEM((8 * 2048, 128), F32),
    pltpu.VMEM((9 * 2048, 128), F32),
    pltpu.VMEM((2, 512, 1024), F32),
    pltpu.VMEM((2, 576, 1024), F32),
    pltpu.VMEM((2, 1, 1024), F32),
    pltpu.VMEM((2, 1, 1024), F32),
    pltpu.VMEM((2, 1, 1024), F32),
    pltpu.VMEM((2, 1, 1024), F32),
    pltpu.VMEM((3, 256, 2048), BF16),
    pltpu.VMEM((2, 256, 576), F32),
    pltpu.VMEM((8, 256, 576), BF16),
    pltpu.VMEM((24, 64, 576), BF16),
    pltpu.VMEM((8, 64, 576), BF16),
    pltpu.VMEM((16, 32, 576), BF16),
    pltpu.VMEM((128, 576), F32),
    pltpu.VMEM((128, 576), BF16),
    pltpu.VMEM((576, 128), F32),
    DMA((3,)), DMA((3,)), DMA((3, 2)), DMA((3, 2)), DMA((3, 3)), DMA((3, 3)), DMA((4, 2)), DMA((4, 2)), DMA((8,)), DMA((8,)),
    DMA((8,)), DMA((8,)), DMA((8, 4)), DMA((24,)), DMA((8, 2)), DMA((16,)), DMA((3,)), DMA((3,)),
]


def hand_over(*refs):
    results, outs, held, sems = refs[:4], refs[4:8], refs[8:12], refs[12]
    loads = [pltpu.make_async_copy(results[i], held[i], sems.at[0, i]) for i in range(4)]
    stores = [pltpu.make_async_copy(held[i], outs[i], sems.at[1, i]) for i in range(4)]
    for load in loads:
        load.start()
    for load, store in zip(loads, stores):
        load.wait()
        store.start()
    for store in stores:
        store.wait()


def body(q_nope, q_rope, latent, up_keys, up_values, out_grad):
    def flat(v):
        return v.reshape(2048, v.shape[2])

    hbm = pl.BlockSpec(memory_space=pl.ANY)
    shapes = [
        jax.ShapeDtypeStruct((2048, 128), BF16),
        jax.ShapeDtypeStruct((2048, 128), BF16),
        jax.ShapeDtypeStruct((16, 64, 128), BF16),
        jax.ShapeDtypeStruct((576, 128), F32),
    ]
    results = pl.pallas_call(
        kernel,
        out_shape=shapes,
        in_specs=[hbm] * 6,
        out_specs=[hbm] * 4,
        scratch_shapes=SCRATCH,
        compiler_params=pltpu.CompilerParams(
            vmem_limit_bytes=63 * 2**20, collective_id=0, has_side_effects=True),
        cost_estimate=pl.CostEstimate(flops=30_000_000_000, bytes_accessed=12_000_000, transcendentals=9_000_000),
    )(latent.T, flat(q_nope), jnp.transpose(q_rope, (1, 2, 0)), flat(out_grad), up_keys, up_values)
    attn, gq, gqr, gl = pl.pallas_call(
        hand_over, out_shape=shapes, in_specs=[hbm] * 4, out_specs=[hbm] * 4,
        scratch_shapes=[pltpu.VMEM(v.shape, v.dtype) for v in shapes] + [DMA((2, 4))],
    )(*results)
    return attn.reshape(128, 16, 128), gq.reshape(128, 16, 128), jnp.transpose(gqr, (2, 0, 1)), gl.T


def solution(mesh):
    rows = P("ctx", "tp", None)
    return jax.shard_map(
        body, mesh=mesh,
        in_specs=(rows, rows, P("ctx", None), P("tp", None, None), P("tp", None, None), rows),
        out_specs=(rows, rows, rows, P("ctx", None)),
        check_vma=False,
    )
```
